256 devices in a mesh: seg: 64 (over y, x, z_lo), chan: 4 (over z_hi, core).
Axes of the slice: x: 4, y: 4, z: 8 (z_hi: 2, z_lo: 4; z = z_hi * 4 + z_lo), core: 2. Of those that a mesh axis runs over, the one named last changes fastest.
Arguments:
- raw: bfloat16 [5120, 262144], P('chan', 'seg'), may hold values from -6 to 6
- fir_taps: bfloat16 [256], replicated, may hold values from -0.375 to 0.375
- band_lo: int32 [1], replicated, may hold values from 4 to 16
- source_chan: int32 [256], replicated, may hold values from 0 to 5119
- dead_chan: int32 [64], replicated, may hold values from 0 to 5119
Outputs:
- stacked: bfloat16 [192, 2, 256, 5120], P('seg', None, None, 'chan')
The draws below stay inside these ranges and needn't reach their ends.
All inputs are finite; a program needn't handle non-finite values.
Results may differ from the reference program's by a relative error of at most 0.0086.
Values may be sent and summed in bfloat16 or wider, within the bound.
A program may use at most 128 MiB of HBM per device.

```python
import math
import jax
import jax.numpy as jnp
from jax import lax

CH = 5120
NFFT = 1024
DEC = 4
TAPS = 256
VS = 256
NDEAD = 64
SEGS = 64
SAMP = 4096
NB = 192


def set_ends(drawn, key, least, largest):
    dims = drawn.shape
    spot = [jax.random.randint(jax.random.fold_in(key, axis), (), 0, dims[axis]) for axis in range(len(dims))]
    drawn = drawn.at[tuple(spot)].set(least)
    longest = dims.index(max(dims))
    spot[longest] = (spot[longest] + 1) % dims[longest]
    return drawn.at[tuple(spot)].set(largest)


def steps_of(rng, extent, shards, low, largest):
    factor_of, own = 1.0, jax.random.fold_in(rng, 6)
    for axis_at, blocks in shards:
        heights = jnp.exp(jax.random.uniform(jax.random.fold_in(own, axis_at), (blocks,), jnp.float32, low / len(shards), largest / len(shards)))
        factor_of = factor_of * jnp.repeat(heights, extent[axis_at] // blocks).reshape([-1 if axis == axis_at else 1 for axis in range(len(extent))])
    return factor_of


def scatter_about(key, dims, spread, reach, shards=(), held_as=jnp.bfloat16):
    entries = spread * jax.random.normal(key, dims, jnp.float32)
    if shards:
        entries = entries * steps_of(key, dims, shards, -0.22, 0.18)
    return jnp.clip(entries, -reach, reach).astype(held_as)


def setup_inputs(seed: int = 0) -> dict:
    key_of = jax.random.split(jax.random.key(seed), 6)
    return {
        "raw": scatter_about(key_of[0], (CH, SEGS * SAMP), 1.0, 6.0, ((0, 4), (1, 64))),
        "fir_taps": scatter_about(key_of[1], (TAPS,), TAPS ** -0.5, 0.375),
        "band_lo": jax.random.randint(key_of[2], (1,), 4, 17).astype(jnp.int32),
        "source_chan": set_ends(jax.random.randint(key_of[3], (VS,), 0, CH), jax.random.fold_in(key_of[3], 1), 0, CH - 1).astype(jnp.int32),
        "dead_chan": set_ends(jax.random.randint(key_of[4], (NDEAD,), 0, CH), jax.random.fold_in(key_of[4], 1), 0, CH - 1).astype(jnp.int32),
    }


def filter_matrix(fir_taps, decim, taps):
    rows = decim * 128 + taps
    row_idx = lax.broadcasted_iota(jnp.int32, (rows, 128), 0)
    col_idx = lax.broadcasted_iota(jnp.int32, (rows, 128), 1)
    tap_idx = decim * col_idx + (decim - 1 + taps) - row_idx
    valid = (tap_idx >= 0) & (tap_idx < taps)
    picked = jnp.take(fir_taps, jnp.clip(tap_idx, 0, taps - 1))
    return jnp.where(valid, picked, jnp.zeros_like(picked))

def dft_table(band_lo, nbins, nfft):
    freq = band_lo[0] + lax.broadcasted_iota(jnp.int32, (nbins, nfft), 0)
    moment = lax.broadcasted_iota(jnp.int32, (nbins, nfft), 1)
    phase = (freq * moment % nfft).astype(jnp.float32) * (2.0 * math.pi / nfft)
    return jnp.concatenate([jnp.cos(phase), -jnp.sin(phase)], axis=0).astype(jnp.bfloat16)

def whiten(spec, alive, nbins):
    real = spec[:nbins]
    imag = spec[nbins:]
    power = real * real + imag * imag
    level = lax.optimization_barrier(jnp.mean(power, axis=0, keepdims=True))
    factor = alive / jnp.sqrt(power + 0.1 * level + 1e-06)
    return jnp.stack([real * factor, imag * factor]).astype(jnp.bfloat16)

def reference(raw, fir_taps, band_lo, source_chan, dead_chan):
    hmat = filter_matrix(fir_taps, DEC, TAPS).astype(jnp.float32)
    table = dft_table(band_lo, NB, NFFT).astype(jnp.float32)
    chan_idx = jnp.arange(CH, dtype=jnp.int32)
    alive = 1.0 - jnp.any(dead_chan[:, None] == chan_idx[None, :], axis=0, keepdims=True).astype(jnp.float32)
    span = hmat.shape[0]
    stride = DEC * 128

    def one_segment(seg_no):
        piece = lax.dynamic_slice_in_dim(raw, (seg_no * SAMP).astype(jnp.int32), SAMP, axis=1)
        start = jnp.maximum(seg_no * SAMP - TAPS, 0).astype(jnp.int32)
        prior = lax.dynamic_slice_in_dim(raw, start, TAPS, axis=1)
        prior = jnp.where(seg_no > 0, prior, jnp.zeros_like(prior))
        extended = jnp.concatenate([prior, piece], axis=1).astype(jnp.float32)
        windows = jnp.stack([extended[:, b * stride:b * stride + span] for b in range(NFFT // 128)], axis=1)
        trace = jnp.einsum('cbi,ij->cbj', windows, hmat).reshape(CH, NFFT).astype(jnp.bfloat16)
        spec = jnp.einsum('kn,cn->kc', table, trace.astype(jnp.float32))
        return whiten(spec, alive, NB)
    white = lax.map(one_segment, jnp.arange(SEGS, dtype=jnp.int32))
    source = white[..., source_chan]
    factor = 1.0 / math.sqrt(SEGS)

    def one_bin(bin_no):
        wbin = lax.dynamic_index_in_dim(white, bin_no, axis=2, keepdims=False).astype(jnp.float32)
        sbin = lax.dynamic_index_in_dim(source, bin_no, axis=2, keepdims=False).astype(jnp.float32)
        real = jnp.einsum('sv,sc->vc', sbin[:, 0], wbin[:, 0]) + jnp.einsum('sv,sc->vc', sbin[:, 1], wbin[:, 1])
        imag = jnp.einsum('sv,sc->vc', sbin[:, 0], wbin[:, 1]) - jnp.einsum('sv,sc->vc', sbin[:, 1], wbin[:, 0])
        return (jnp.stack([real, imag]) * factor).astype(jnp.bfloat16)
    return lax.map(one_bin, jnp.arange(NB, dtype=jnp.int32))
```

```python
import functools
import math

import jax
import jax.numpy as jnp
from jax import lax
from jax.experimental import pallas as pl
from jax.experimental.pallas import tpu as pltpu
from jax.sharding import PartitionSpec as P

NFFT = 1024
DEC = 4
TAPS = 256
BIN_DEV = 3
LANE = 128
BLOCK = 256
SPAN = DEC * BLOCK + TAPS
CHUNKS = ((0, 384), (384, 384), (768, 256), (1024, 256))
MAIN = (0, 1, 3, 4, 6, 7, 8, 9)
SPARE = ((2, 0), (2, 1), (2, 2), (5, 0), (5, 1), (5, 2), None, None)
MESH = pl.DeviceIdType.MESH


def fir_matrix(base_ref, hmat):
    rolled = pltpu.roll(
        jnp.broadcast_to(base_ref[...], (64, 512)), 0, 1, stride=DEC, stride_axis=0
    )
    rows = []
    for part in range(BLOCK // 64):
        pieces = []
        if part:
            pieces.append(jnp.zeros((64, 256 * part), jnp.float32))
        pieces.append(rolled)
        if part < 3:
            pieces.append(jnp.zeros((64, 256 * (3 - part)), jnp.float32))
        rows.append(jnp.concatenate(pieces, axis=1))
    hmat[...] = jnp.concatenate(rows, axis=0).T.astype(jnp.bfloat16)


def dft_table(band_ref, table, nseg):
    def block(i, _):
        row = i * 64 + lax.broadcasted_iota(jnp.int32, (64, LANE), 0)
        lane = lax.broadcasted_iota(jnp.int32, (64, LANE), 1)
        part = (row >> 2) & 1
        which = row & 3
        freq = band_ref[0] + BIN_DEV * (row >> 3) + which
        live = which < BIN_DEV

        def unit(turn):
            turn = turn & (NFFT - 1)
            quad = ((turn + 128) >> 8) & 3
            rest = ((turn + 128) & 255) - 128
            x = rest.astype(jnp.float32) * (2.0 * math.pi / NFFT)
            x2 = x * x
            sin = x * (1.0 + x2 * (-1.0 / 6 + x2 * (1.0 / 120 + x2 * (-1.0 / 5040 + x2 / 362880))))
            cos = 1.0 + x2 * (
                -0.5 + x2 * (1.0 / 24 + x2 * (-1.0 / 720 + x2 * (1.0 / 40320 - x2 / 3628800)))
            )
            swap = (quad & 1) == 1
            c = jnp.where(swap, sin, cos)
            s = jnp.where(swap, cos, sin)
            c = jnp.where((quad == 1) | (quad == 2), -c, c)
            s = jnp.where(quad >= 2, -s, s)
            return c, s

        c, s = unit(freq * lane + 256 * part)
        cr, sr = unit(freq * LANE)
        c = jnp.where(live, c, 0.0)
        s = jnp.where(live, s, 0.0)
        for a in range(NFFT // LANE):
            table[pl.ds(pl.multiple_of(i * 64, 64), 64), a * LANE : (a + 1) * LANE] = c.astype(
                jnp.bfloat16
            )
            c, s = c * cr - s * sr, s * cr + c * sr
        return 0

    lax.fori_loop(0, nseg // 8, block, 0)


def kernel(
    nseg,
    raw,
    base_ref,
    band_ref,
    src_ref,
    dead_ref,
    right_ref,
    left_ref,
    xbuf,
    tail,
    trace,
    first,
    hmat,
    table,
    halo_out,
    halo_in,
    spec,
    fill,
    outbox,
    inbox,
    wide,
    picked,
    half_in,
    half_sum,
    far_in,
    total,
    tail_sem,
    raw_sem,
    halo_send,
    halo_recv,
    box_send,
    box_recv,
    ex_send,
    ex_recv,
):
    seg = lax.axis_index("seg")
    chan = lax.axis_index("chan")
    chans = raw.shape[0]
    samples = raw.shape[1]
    core = chan & 1
    sibling = {"chan": chan ^ 1}
    far = {"chan": chan ^ 2}
    nextseg = {"seg": lax.rem(seg + 1, nseg)}

    tail_copy = pltpu.make_async_copy(raw.at[:, pl.ds(samples - TAPS, TAPS)], tail, tail_sem)
    tail_copy.start()
    raw_copies = [
        pltpu.make_async_copy(
            raw.at[pl.ds(i * BLOCK, BLOCK)], xbuf.at[pl.ds(i * BLOCK, BLOCK)], raw_sem.at[i]
        )
        for i in range(chans // BLOCK)
    ]
    for copy in raw_copies:
        copy.start()

    barrier = pltpu.get_barrier_semaphore()

    @pl.loop(1, nseg)
    def _(d):
        pl.semaphore_signal(
            barrier, 1, device_id={"seg": lax.rem(seg + d, nseg)}, device_id_type=MESH
        )

    pl.semaphore_signal(barrier, 1, device_id=sibling, device_id_type=MESH)
    pl.semaphore_signal(barrier, 1, device_id=far, device_id_type=MESH)

    fir_matrix(base_ref, hmat)
    tail_copy.wait()
    lane64 = lax.broadcasted_iota(jnp.int32, (1, LANE), 1) < 64
    near = hmat[0:TAPS, 0:LANE]
    near = jnp.where(lane64, near.astype(jnp.float32), 0.0)
    low = near.astype(jnp.bfloat16)
    high = pltpu.roll(near, 64, 1).astype(jnp.bfloat16)
    for c0, w in CHUNKS:
        h = w // 2
        part = jnp.dot(tail[c0 : c0 + h], low, preferred_element_type=jnp.float32) + jnp.dot(
            tail[c0 + h : c0 + w], high, preferred_element_type=jnp.float32
        )
        halo_out[c0 // 2 : c0 // 2 + h] = part.astype(jnp.bfloat16)

    dft_table(band_ref, table, nseg)
    pl.semaphore_wait(barrier, nseg + 1)
    halos = []
    for q, (c0, w) in enumerate(CHUNKS):
        rows = pl.ds(c0 // 2, w // 2)
        copy = pltpu.make_async_remote_copy(
            halo_out.at[rows],
            halo_in.at[rows],
            halo_send.at[q],
            halo_recv.at[q],
            device_id=nextseg,
            device_id_type=MESH,
        )
        copy.start()
        halos.append(copy)

    chan_row = chan * chans + lax.broadcasted_iota(jnp.int32, (1, chans), 1)

    def mark(i, hit):
        return jnp.where(chan_row == dead_ref[i], 0.0, hit)

    alive = lax.fori_loop(0, dead_ref.shape[0], mark, jnp.ones((1, chans), jnp.float32))

    for i in range(chans // BLOCK):
        rows = slice(i * BLOCK, (i + 1) * BLOCK)
        raw_copies[i].wait()
        for b in range(NFFT // BLOCK):
            begin = b * DEC * BLOCK - TAPS
            if b == 0:
                acc = jnp.dot(
                    xbuf[rows, 0 : DEC * BLOCK], hmat[TAPS:], preferred_element_type=jnp.float32
                )
                first[rows] = acc[:, :LANE]
                trace[rows, LANE:BLOCK] = acc[:, LANE:].astype(jnp.bfloat16)
            else:
                acc = jnp.dot(
                    xbuf[rows, begin : begin + SPAN], hmat[...], preferred_element_type=jnp.float32
                )
                trace[rows, b * BLOCK : (b + 1) * BLOCK] = acc.astype(jnp.bfloat16)

    has_prior = jnp.where(seg > 0, 1.0, 0.0)
    spare_row = (lax.broadcasted_iota(jnp.int32, (1, 8, 1), 1) & 3) == 3
    for q, (c0, w) in enumerate(CHUNKS):
        h = w // 2
        halos[q].wait_recv()
        prior = halo_in[c0 // 2 : c0 // 2 + h].astype(jnp.float32) * has_prior
        prior_low = jnp.where(lane64, prior, 0.0)
        prior_high = jnp.where(lane64, pltpu.roll(prior, 64, 1), 0.0)
        trace[c0 : c0 + h, 0:LANE] = (first[c0 : c0 + h] + prior_low).astype(jnp.bfloat16)
        trace[c0 + h : c0 + w, 0:LANE] = (first[c0 + h : c0 + w] + prior_high).astype(jnp.bfloat16)
        spec[:, :w] = lax.dot_general(
            table[...],
            trace[c0 : c0 + w],
            (((1,), (1,)), ((), ())),
            preferred_element_type=jnp.float32,
        )

        def square(i, acc, w=w):
            s = spec[pl.ds(pl.multiple_of(i * 64, 64), 64), :w].reshape(8, 8, w)
            return acc + jnp.sum(s * s, axis=0)

        energy = lax.fori_loop(0, nseg // 8, square, jnp.zeros((8, w), jnp.float32))
        level = jnp.sum(energy, axis=0, keepdims=True) * (1.0 / (BIN_DEV * nseg))
        floor = (0.1 * level + 1e-6).reshape(1, 1, w)
        live = alive[:, c0 : c0 + w].reshape(1, 1, w)

        def white(i, _, w=w, q=q, floor=floor, live=live):
            dest = pl.ds(i * 8, 8)
            s = spec[pl.ds(pl.multiple_of(i * 64, 64), 64), :w].reshape(8, 8, w)
            sq = s * s
            power = sq + pltpu.roll(sq, 4, 1)
            out = s * (live * lax.rsqrt(power + floor))
            one = out[:, :, 0:LANE]
            two = out[:, :, LANE : 2 * LANE]
            if q == 0:
                extra = out[:, :, 2 * LANE :]
                one = jnp.where(spare_row, pltpu.roll(extra, 3, 1), one)
                two = jnp.where(spare_row, pltpu.roll(extra, 2, 1), two)
                fill[0, dest] = pltpu.roll(extra, 1, 1)
            elif q == 1:
                extra = out[:, :, 2 * LANE :]
                one = jnp.where(spare_row, fill[0, dest], one)
                two = jnp.where(spare_row, pltpu.roll(extra, 3, 1), two)
                fill[1, dest] = pltpu.roll(extra, 2, 1)
                fill[2, dest] = pltpu.roll(extra, 1, 1)
            elif q == 2:
                one = jnp.where(spare_row, fill[1, dest], one)
                two = jnp.where(spare_row, fill[2, dest], two)
            outbox[q, dest] = jnp.concatenate([one, two], axis=1).astype(jnp.bfloat16)
            return 0

        lax.fori_loop(0, nseg // 8, white, 0)

        pltpu.make_async_copy(outbox.at[q, seg], inbox.at[q, seg], box_recv.at[q]).start()

        @pl.loop(1, nseg)
        def _(d, q=q):
            to = lax.rem(seg + d, nseg)
            pltpu.make_async_remote_copy(
                outbox.at[q, to],
                inbox.at[q, seg],
                box_send.at[q],
                box_recv.at[q],
                device_id={"seg": to},
                device_id_type=MESH,
            ).start()

    for q in range(len(CHUNKS)):
        pltpu.make_async_copy(inbox.at[q], inbox.at[q], box_recv.at[q]).wait()
        wide[...] = inbox[q].reshape(nseg * 16, LANE).astype(jnp.float32)
        for slab in range(2):
            at = 2 * q + slab
            for i in range(8):
                part, which = i // 4, i % 4
                group = MAIN[at]
                if which == 3:
                    if SPARE[at] is None:
                        continue
                    group, which = SPARE[at]
                rows = wide[pl.ds(slab * 8 + i, nseg, stride=16), :]
                right_ref[
                    which, part * nseg : (part + 1) * nseg, group * LANE : (group + 1) * LANE
                ] = rows.astype(jnp.bfloat16)

    here = chan * chans
    for b in range(BIN_DEV):
        acc = jnp.zeros((2 * nseg, src_ref.shape[1]), jnp.float32)
        for c0 in range(0, chans, BLOCK):
            ids = here + c0 + lax.broadcasted_iota(jnp.int32, (BLOCK, src_ref.shape[1]), 0)
            hot = jnp.where(ids == src_ref[...], 1.0, 0.0).astype(jnp.bfloat16)
            acc += jnp.dot(
                right_ref[b, :, c0 : c0 + BLOCK], hot, preferred_element_type=jnp.float32
            )
        acc = acc.astype(jnp.bfloat16)
        picked[b, 0] = acc[:nseg]
        picked[b, 1] = acc[nseg:]

    def exchange(step, b, src, dst, to):
        copy = pltpu.make_async_remote_copy(
            src,
            dst,
            ex_send.at[step, b],
            ex_recv.at[step, b],
            device_id=to,
            device_id_type=MESH,
        )
        copy.start()
        return copy

    other = 1 - core
    steps = [[exchange(0, b, picked.at[b, other], half_in.at[b], sibling) for b in range(BIN_DEV)]]
    steps.append([])
    for b in range(BIN_DEV):
        steps[0][b].wait_recv()
        half_sum[b] = picked[b, core] + half_in[b]
        steps[1].append(exchange(1, b, half_sum.at[b], far_in.at[b], far))
    steps.append([])
    for b in range(BIN_DEV):
        steps[1][b].wait_recv()
        total[b, core] = half_sum[b] + far_in[b]
        steps[2].append(exchange(2, b, total.at[b, core], total.at[b, core], sibling))
    for b in range(BIN_DEV):
        steps[2][b].wait_recv()
        left_ref[b, :nseg] = total[b, 0]
        left_ref[b, nseg:] = total[b, 1]
    for step in steps:
        for copy in step:
            copy.wait_send()
    for copy in halos:
        copy.wait_send()
    for q in range(len(CHUNKS)):
        sent = outbox.at[q, pl.ds(0, nseg - 1)]
        pltpu.make_async_copy(sent, sent, box_send.at[q]).wait()


def correlate_kernel(factor, left_ref, right_ref, out_ref):
    half = left_ref.shape[1] // 2
    right = right_ref[0]
    left = left_ref[0] * jnp.bfloat16(factor)
    turned = jnp.concatenate([-left[half:], left[:half]], axis=0)
    for part, lhs in enumerate((left, turned)):
        out_ref[0, part] = lax.dot_general(
            lhs, right, (((0,), (0,)), ((), ())), preferred_element_type=jnp.float32
        ).astype(jnp.bfloat16)


def per_device(nseg, raw, fir_taps, band_lo, source_chan, dead_chan):
    chans = raw.shape[0]
    nsrc = source_chan.shape[0]
    base = jnp.pad(fir_taps[::-1].astype(jnp.float32), (DEC, 512 - TAPS - DEC)).reshape(1, 512)
    vmem = pl.BlockSpec(memory_space=pltpu.VMEM)
    smem = pl.BlockSpec(memory_space=pltpu.SMEM)
    bf16, f32 = jnp.bfloat16, jnp.float32
    nq = len(CHUNKS)
    right, left = pl.pallas_call(
        functools.partial(kernel, nseg),
        out_shape=(
            jax.ShapeDtypeStruct((BIN_DEV, 2 * nseg, chans), bf16),
            jax.ShapeDtypeStruct((BIN_DEV, 2 * nseg, nsrc), bf16),
        ),
        in_specs=[pl.BlockSpec(memory_space=pl.ANY), vmem, smem, vmem, smem],
        out_specs=(vmem, vmem),
        scratch_shapes=[
            pltpu.VMEM(raw.shape, bf16),
            pltpu.VMEM((chans, TAPS), bf16),
            pltpu.VMEM((chans, NFFT), bf16),
            pltpu.VMEM((chans, LANE), f32),
            pltpu.VMEM((SPAN, BLOCK), bf16),
            pltpu.VMEM((8 * nseg, NFFT), bf16),
            pltpu.VMEM((chans // 2, LANE), bf16),
            pltpu.VMEM((chans // 2, LANE), bf16),
            pltpu.VMEM((8 * nseg, 384), f32),
            pltpu.VMEM((3, nseg, 8, LANE), f32),
            pltpu.VMEM((nq, nseg, 16, LANE), bf16),
            pltpu.VMEM((nq, nseg, 16, LANE), bf16),
            pltpu.VMEM((nseg * 16, LANE), f32),
            pltpu.VMEM((BIN_DEV, 2, nseg, nsrc), bf16),
            pltpu.VMEM((BIN_DEV, nseg, nsrc), bf16),
            pltpu.VMEM((BIN_DEV, nseg, nsrc), bf16),
            pltpu.VMEM((BIN_DEV, nseg, nsrc), bf16),
            pltpu.VMEM((BIN_DEV, 2, nseg, nsrc), bf16),
            pltpu.SemaphoreType.DMA,
            pltpu.SemaphoreType.DMA((chans // BLOCK,)),
            pltpu.SemaphoreType.DMA((nq,)),
            pltpu.SemaphoreType.DMA((nq,)),
            pltpu.SemaphoreType.DMA((nq,)),
            pltpu.SemaphoreType.DMA((nq,)),
            pltpu.SemaphoreType.DMA((3, BIN_DEV)),
            pltpu.SemaphoreType.DMA((3, BIN_DEV)),
        ],
        compiler_params=pltpu.CompilerParams(
            collective_id=0, has_side_effects=True, vmem_limit_bytes=48 * 1024 * 1024
        ),
        name="whiten_exchange",
    )(raw, base, band_lo, source_chan.reshape(1, nsrc), dead_chan)
    return pl.pallas_call(
        functools.partial(correlate_kernel, 1.0 / math.sqrt(nseg)),
        grid=(BIN_DEV,),
        out_shape=jax.ShapeDtypeStruct((BIN_DEV, 2, nsrc, chans), bf16),
        in_specs=[
            pl.BlockSpec((1, 2 * nseg, nsrc), lambda b: (b, 0, 0)),
            pl.BlockSpec((1, 2 * nseg, chans), lambda b: (b, 0, 0)),
        ],
        out_specs=pl.BlockSpec((1, 2, nsrc, chans), lambda b: (b, 0, 0, 0)),
        compiler_params=pltpu.CompilerParams(vmem_limit_bytes=32 * 1024 * 1024),
        name="correlate",
    )(left, right)


def solution(mesh):
    return jax.shard_map(
        functools.partial(per_device, mesh.shape["seg"]),
        mesh=mesh,
        in_specs=(P("chan", "seg"), P(), P(), P(), P()),
        out_specs=P("seg", None, None, "chan"),
        check_vma=False,
    )
```

```python
import functools
import math

import jax
import jax.numpy as jnp
from jax import lax
from jax.experimental import pallas as pl
from jax.experimental.pallas import tpu as pltpu
from jax.sharding import PartitionSpec as P

NFFT = 1024
DEC = 4
TAPS = 256
BINS = 3
LANE = 128
BLOCK = 256
SPAN = DEC * BLOCK + TAPS
CHUNKS = ((1024, 256), (0, 512), (512, 512))
ROWS = 16
MESH = pl.DeviceIdType.MESH


def box_row(part, b, group):
    if group < 8:
        return 1 + b, 8 * part + group
    return 0, 8 * part + 2 * b + group - 8


def fir_rows(taps):
    tap_no = lax.broadcasted_iota(jnp.int32, (TAPS, 512), 0)
    place = lax.broadcasted_iota(jnp.int32, (TAPS, 512), 1)
    onehot = jnp.where(tap_no + place == TAPS + DEC - 1, 1.0, 0.0).astype(jnp.bfloat16)
    base = jnp.dot(
        jnp.broadcast_to(taps, (64, TAPS)).astype(jnp.bfloat16),
        onehot,
        preferred_element_type=jnp.float32,
    )
    return pltpu.roll(base, 0, 1, stride=DEC, stride_axis=0)


def fir_matrix(rolled):
    rows = []
    for part in range(BLOCK // 64):
        pieces = []
        if part:
            pieces.append(jnp.zeros((64, 256 * part), jnp.float32))
        pieces.append(rolled)
        if part < 3:
            pieces.append(jnp.zeros((64, 256 * (3 - part)), jnp.float32))
        rows.append(jnp.concatenate(pieces, axis=1))
    return jnp.concatenate(rows, axis=0).T.astype(jnp.bfloat16)


def dft_table(band_ref, table, nseg):
    def block(i, _):
        part = i // BINS
        freq = band_ref[0] + i % BINS + BINS * lax.broadcasted_iota(jnp.int32, (nseg, LANE), 0)
        lane = lax.broadcasted_iota(jnp.int32, (nseg, LANE), 1)

        def unit(turn):
            turn = turn & (NFFT - 1)
            quad = ((turn + 128) >> 8) & 3
            rest = ((turn + 128) & 255) - 128
            x = rest.astype(jnp.float32) * (2.0 * math.pi / NFFT)
            x2 = x * x
            sin = x * (1.0 + x2 * (-1.0 / 6 + x2 * (1.0 / 120 + x2 * (-1.0 / 5040 + x2 / 362880))))
            cos = 1.0 + x2 * (
                -0.5 + x2 * (1.0 / 24 + x2 * (-1.0 / 720 + x2 * (1.0 / 40320 - x2 / 3628800)))
            )
            swap = (quad & 1) == 1
            c = jnp.where(swap, sin, cos)
            s = jnp.where(swap, cos, sin)
            c = jnp.where((quad == 1) | (quad == 2), -c, c)
            s = jnp.where(quad >= 2, -s, s)
            return c, s

        c, s = unit(freq * lane + 256 * part)
        cr, sr = unit(freq * LANE)
        for a in range(NFFT // LANE):
            rows = pl.ds(pl.multiple_of(i * nseg, nseg), nseg)
            table[rows, a * LANE : (a + 1) * LANE] = c.astype(jnp.bfloat16)
            c, s = c * cr - s * sr, s * cr + c * sr
        return 0

    lax.fori_loop(0, 2 * BINS, block, 0)


def products(left, right, factor):
    half = left.shape[0] // 2
    left = left * jnp.bfloat16(factor)
    turned = jnp.concatenate([-left[half:], left[:half]], axis=0)
    return [
        lax.dot_general(
            lhs, right, (((0,), (0,)), ((), ())), preferred_element_type=jnp.float32
        ).astype(jnp.bfloat16)
        for lhs in (left, turned)
    ]


def kernel(
    nseg,
    factor,
    nsrc,
    ndead,
    raw,
    small_ref,
    band_ref,
    done_ref,
    right_last,
    left_last,
    hot,
    xbuf,
    tail,
    trace,
    first,
    hmat,
    table,
    halo_out,
    halo_in,
    spec,
    tiles,
    outbox,
    inbox,
    wide,
    right_ref,
    picked,
    half_in,
    half_sum,
    far_in,
    total,
    tail_sem,
    raw_sem,
    halo_send,
    halo_recv,
    box_send,
    box_recv,
    ex_send,
    ex_recv,
):
    seg = lax.axis_index("seg")
    chan = lax.axis_index("chan")
    chans = raw.shape[0]
    samples = raw.shape[1]
    core = chan & 1
    sibling = {"chan": chan ^ 1}
    far = {"chan": chan ^ 2}
    nextseg = {"seg": lax.rem(seg + 1, nseg)}

    tail_copy = pltpu.make_async_copy(raw.at[:, pl.ds(samples - TAPS, TAPS)], tail, tail_sem)
    raw_copies = [
        pltpu.make_async_copy(raw.at[pl.ds(c0, w)], xbuf.at[pl.ds(c0, w)], raw_sem.at[q])
        for q, (c0, w) in enumerate(CHUNKS)
    ]
    for copy in (tail_copy, raw_copies[0], raw_copies[1]):
        copy.start()

    barrier = pltpu.get_barrier_semaphore()

    @pl.loop(1, nseg)
    def _(d):
        pl.semaphore_signal(
            barrier, 1, device_id={"seg": lax.rem(seg + d, nseg)}, device_id_type=MESH
        )

    pl.semaphore_signal(barrier, 1, device_id=sibling, device_id_type=MESH)
    pl.semaphore_signal(barrier, 1, device_id=far, device_id_type=MESH)

    rolled = fir_rows(small_ref[:, :TAPS])
    lane64 = lax.broadcasted_iota(jnp.int32, (1, LANE), 1) < 64
    near = rolled[:, :TAPS]
    low = jnp.concatenate([near, jnp.zeros_like(near)], axis=0).astype(jnp.bfloat16)
    high = jnp.concatenate([jnp.zeros_like(near), near], axis=0).astype(jnp.bfloat16)
    over_time = (((1,), (1,)), ((), ()))
    tail_copy.wait()
    for c0, w in CHUNKS:
        h = w // 2
        part = lax.dot_general(
            tail[c0 : c0 + h], low, over_time, preferred_element_type=jnp.float32
        ) + lax.dot_general(
            tail[c0 + h : c0 + w], high, over_time, preferred_element_type=jnp.float32
        )
        halo_out[c0 // 2 : c0 // 2 + h] = part.astype(jnp.bfloat16)

    pl.semaphore_wait(barrier, nseg + 1)
    halos = []
    for q, (c0, w) in enumerate(CHUNKS):
        rows = pl.ds(c0 // 2, w // 2)
        copy = pltpu.make_async_remote_copy(
            halo_out.at[rows],
            halo_in.at[rows],
            halo_send.at[q],
            halo_recv.at[q],
            device_id=nextseg,
            device_id_type=MESH,
        )
        copy.start()
        halos.append(copy)

    hmat[...] = fir_matrix(rolled)

    def filtered(q):
        c0, w = CHUNKS[q]
        rows = slice(c0, c0 + w)
        raw_copies[q].wait()
        if q + 2 < len(CHUNKS):
            raw_copies[q + 2].start()
        for b in range(NFFT // BLOCK):
            begin = b * DEC * BLOCK - TAPS
            if b == 0:
                acc = jnp.dot(
                    xbuf[rows, 0 : DEC * BLOCK], hmat[TAPS:], preferred_element_type=jnp.float32
                )
                first[rows] = acc[:, :LANE]
                trace[rows, LANE:BLOCK] = acc[:, LANE:].astype(jnp.bfloat16)
            else:
                acc = jnp.dot(
                    xbuf[rows, begin : begin + SPAN], hmat[...], preferred_element_type=jnp.float32
                )
                trace[rows, b * BLOCK : (b + 1) * BLOCK] = acc.astype(jnp.bfloat16)

    filtered(0)
    dft_table(band_ref, table, nseg)

    first_chan = (chan * chans).astype(jnp.float32)
    padded = small_ref[:, TAPS + nsrc :]
    dead = jnp.broadcast_to(padded, (LANE, LANE)).T[:ndead]
    lane = lax.broadcasted_iota(jnp.int32, (1, LANE), 1).astype(jnp.float32)
    alive = []
    for c0 in range(0, chans, LANE):
        hits = jnp.where(dead == lane + (first_chan + c0), 1.0, 0.0)
        alive.append(1.0 - jnp.max(hits, axis=0, keepdims=True))
    has_prior = jnp.where(seg > 0, 1.0, 0.0)
    nothing = jnp.zeros((nseg, LANE), jnp.float32)
    for row in (6, 7, 14, 15):
        tiles[0, pl.ds(row, nseg, stride=ROWS), :] = nothing

    def post(box):
        outbox[box] = tiles[box].reshape(nseg, ROWS, LANE).astype(jnp.bfloat16)
        pltpu.make_async_copy(outbox.at[box, seg], inbox.at[box, seg], box_recv.at[box]).start()

        @pl.loop(1, nseg)
        def _(d):
            to = lax.rem(seg + d, nseg)
            pltpu.make_async_remote_copy(
                outbox.at[box, to],
                inbox.at[box, seg],
                box_send.at[box],
                box_recv.at[box],
                device_id={"seg": to},
                device_id_type=MESH,
            ).start()

    for q, (c0, w) in enumerate(CHUNKS):
        h = w // 2
        halos[q].wait_recv()
        prior = halo_in[c0 // 2 : c0 // 2 + h].astype(jnp.float32) * has_prior
        prior_low = jnp.where(lane64, prior, 0.0)
        prior_high = jnp.where(lane64, pltpu.roll(prior, 64, 1), 0.0)
        trace[c0 : c0 + h, 0:LANE] = (first[c0 : c0 + h] + prior_low).astype(jnp.bfloat16)
        trace[c0 + h : c0 + w, 0:LANE] = (first[c0 + h : c0 + w] + prior_high).astype(jnp.bfloat16)
        spec[:, :w] = lax.dot_general(
            table[...], trace[c0 : c0 + w], over_time, preferred_element_type=jnp.float32
        )
        for at in range(0, w, LANE):
            lanes = slice(at, at + LANE)
            group = (c0 + at) // LANE
            energy = jnp.zeros((8, LANE), jnp.float32)
            for row in range(2 * BINS):
                s = spec[row * nseg : (row + 1) * nseg, lanes].reshape(nseg // 8, 8, LANE)
                energy += jnp.sum(s * s, axis=0)
            level = jnp.sum(energy, axis=0, keepdims=True) * (1.0 / (BINS * nseg))
            live = alive[group]
            for b in range(BINS):
                real = spec[b * nseg : (b + 1) * nseg, lanes]
                imag = spec[(BINS + b) * nseg : (BINS + b + 1) * nseg, lanes]
                gain = live * lax.rsqrt(real * real + imag * imag + (0.1 * level + 1e-6))
                for part, value in enumerate((real, imag)):
                    box, row = box_row(part, b, group)
                    tiles[box, pl.ds(row, nseg, stride=ROWS), :] = value * gain
        if q == 0:
            post(0)
            filtered(1)
        elif q == 1:
            filtered(2)
    for b in range(BINS):
        post(1 + b)

    source = small_ref[:, TAPS : TAPS + nsrc]
    for c0 in range(0, chans, LANE):
        ids = lax.broadcasted_iota(jnp.int32, (LANE, nsrc), 0).astype(jnp.float32)
        hot[c0 : c0 + LANE] = jnp.where(ids + (first_chan + c0) == source, 1.0, 0.0).astype(
            jnp.bfloat16
        )

    def right_of(b):
        return right_last if b == BINS - 1 else right_ref.at[b]

    def collect(box):
        pltpu.make_async_copy(inbox.at[box], inbox.at[box], box_recv.at[box]).wait()
        wide[...] = inbox[box].reshape(nseg * ROWS, LANE).astype(jnp.float32)
        for part in range(2):
            for b in range(BINS):
                for group in range(chans // LANE):
                    held, row = box_row(part, b, group)
                    if held == box:
                        right_of(b)[
                            part * nseg : (part + 1) * nseg, group * LANE : (group + 1) * LANE
                        ] = wide[pl.ds(row, nseg, stride=ROWS), :].astype(jnp.bfloat16)

    copies = {}

    def exchange(step, b, src, dst, to):
        copy = pltpu.make_async_remote_copy(
            src,
            dst,
            ex_send.at[step, b],
            ex_recv.at[step, b],
            device_id=to,
            device_id_type=MESH,
        )
        copy.start()
        copies[step, b] = copy

    def step_pick(b):
        acc = jnp.dot(right_of(b)[...], hot[...], preferred_element_type=jnp.float32)
        acc = acc.astype(jnp.bfloat16)
        picked[b, 0] = acc[:nseg]
        picked[b, 1] = acc[nseg:]
        exchange(0, b, picked.at[b, 1 - core], half_in.at[b], sibling)

    def step_far(b):
        copies[0, b].wait_recv()
        half_sum[b] = picked[b, core] + half_in[b]
        exchange(1, b, half_sum.at[b], far_in.at[b], far)

    def step_back(b):
        copies[1, b].wait_recv()
        total[b, core] = half_sum[b] + far_in[b]
        exchange(2, b, total.at[b, core], total.at[b, core], sibling)

    def step_product(b):
        copies[2, b].wait_recv()
        left = jnp.concatenate([total[b, 0], total[b, 1]], axis=0)
        if b == BINS - 1:
            left_last[...] = left
            return
        for part, value in enumerate(products(left, right_ref[b], factor)):
            done_ref[b, part] = value

    collect(0)
    collect(1)
    step_pick(0)
    collect(2)
    step_pick(1)
    step_far(0)
    collect(3)
    step_pick(2)
    step_far(1)
    step_far(2)
    for b in range(BINS):
        step_back(b)
    for b in range(BINS):
        step_product(b)
    for copy in copies.values():
        copy.wait_send()
    for copy in halos:
        copy.wait_send()
    for box in range(outbox.shape[0]):
        sent = outbox.at[box, pl.ds(0, nseg - 1)]
        pltpu.make_async_copy(sent, sent, box_send.at[box]).wait()


def finish_kernel(factor, done_ref, right_ref, left_ref, out_ref, buf, sems):
    last = BINS - 1
    copies = [pltpu.make_async_copy(done_ref, out_ref.at[pl.ds(0, last)], sems.at[2])]
    copies[0].start()
    for part, value in enumerate(products(left_ref[...], right_ref[...], factor)):
        buf[part] = value
        copy = pltpu.make_async_copy(buf.at[part], out_ref.at[last, part], sems.at[part])
        copy.start()
        copies.append(copy)
    for copy in copies:
        copy.wait()


def per_device(nseg, raw, fir_taps, band_lo, source_chan, dead_chan):
    chans = raw.shape[0]
    nsrc = source_chan.shape[0]
    ndead = dead_chan.shape[0]
    factor = 1.0 / math.sqrt(nseg)
    vmem = pl.BlockSpec(memory_space=pltpu.VMEM)
    smem = pl.BlockSpec(memory_space=pltpu.SMEM)
    hbm = pl.BlockSpec(memory_space=pltpu.HBM)
    bf16, f32 = jnp.bfloat16, jnp.float32
    small = jnp.concatenate(
        [x.astype(f32) for x in (fir_taps, source_chan, dead_chan)]
        + [jnp.full((LANE - ndead,), -1.0, f32)]
    ).reshape(1, TAPS + nsrc + LANE)
    nq = len(CHUNKS)
    nbox = 1 + BINS
    done, right, left = pl.pallas_call(
        functools.partial(kernel, nseg, factor, nsrc, ndead),
        out_shape=(
            jax.ShapeDtypeStruct((BINS - 1, 2, nsrc, chans), bf16),
            jax.ShapeDtypeStruct((2 * nseg, chans), bf16),
            jax.ShapeDtypeStruct((2 * nseg, nsrc), bf16),
        ),
        in_specs=[hbm, vmem, smem],
        out_specs=(vmem, vmem, vmem),
        scratch_shapes=[
            pltpu.VMEM((chans, nsrc), bf16),
            pltpu.VMEM(raw.shape, bf16),
            pltpu.VMEM((chans, TAPS), bf16),
            pltpu.VMEM((chans, NFFT), bf16),
            pltpu.VMEM((chans, LANE), f32),
            pltpu.VMEM((SPAN, BLOCK), bf16),
            pltpu.VMEM((2 * BINS * nseg, NFFT), bf16),
            pltpu.VMEM((chans // 2, LANE), bf16),
            pltpu.VMEM((chans // 2, LANE), bf16),
            pltpu.VMEM((2 * BINS * nseg, 512), f32),
            pltpu.VMEM((nbox, nseg * ROWS, LANE), f32),
            pltpu.VMEM((nbox, nseg, ROWS, LANE), bf16),
            pltpu.VMEM((nbox, nseg, ROWS, LANE), bf16),
            pltpu.VMEM((nseg * ROWS, LANE), f32),
            pltpu.VMEM((BINS - 1, 2 * nseg, chans), bf16),
            pltpu.VMEM((BINS, 2, nseg, nsrc), bf16),
            pltpu.VMEM((BINS, nseg, nsrc), bf16),
            pltpu.VMEM((BINS, nseg, nsrc), bf16),
            pltpu.VMEM((BINS, nseg, nsrc), bf16),
            pltpu.VMEM((BINS, 2, nseg, nsrc), bf16),
            pltpu.SemaphoreType.DMA,
            pltpu.SemaphoreType.DMA((nq,)),
            pltpu.SemaphoreType.DMA((nq,)),
            pltpu.SemaphoreType.DMA((nq,)),
            pltpu.SemaphoreType.DMA((nbox,)),
            pltpu.SemaphoreType.DMA((nbox,)),
            pltpu.SemaphoreType.DMA((3, BINS)),
            pltpu.SemaphoreType.DMA((3, BINS)),
        ],
        compiler_params=pltpu.CompilerParams(
            collective_id=0, has_side_effects=True, vmem_limit_bytes=44 * 1024 * 1024
        ),
        name="whiten_exchange",
    )(raw, small, band_lo)
    return pl.pallas_call(
        functools.partial(finish_kernel, factor),
        out_shape=jax.ShapeDtypeStruct((BINS, 2, nsrc, chans), bf16),
        in_specs=[vmem, vmem, vmem],
        out_specs=hbm,
        scratch_shapes=[
            pltpu.VMEM((2, nsrc, chans), bf16),
            pltpu.SemaphoreType.DMA((3,)),
        ],
        compiler_params=pltpu.CompilerParams(vmem_limit_bytes=32 * 1024 * 1024),
        name="finish",
    )(done, right, left)


def solution(mesh):
    return jax.shard_map(
        functools.partial(per_device, mesh.shape["seg"]),
        mesh=mesh,
        in_specs=(P("chan", "seg"), P(), P(), P(), P()),
        out_specs=P("seg", None, None, "chan"),
        check_vma=False,
    )
```

```python
import functools
import math

import jax
import jax.numpy as jnp
from jax import lax
from jax.experimental import pallas as pl
from jax.experimental.pallas import tpu as pltpu
from jax.sharding import PartitionSpec as P

NFFT = 1024
DEC = 4
TAPS = 256
BINS = 3
LANE = 128
BLOCK = 256
SPAN = DEC * BLOCK + TAPS
CHUNKS = ((1024, 256), (0, 512), (512, 512))
ROWS = 16
MESH = pl.DeviceIdType.MESH


def box_row(part, b, group):
    if group < 8:
        return 1 + b, 8 * part + group
    return 0, 8 * part + 2 * b + group - 8


def fir_rows(taps):
    tap_no = lax.broadcasted_iota(jnp.int32, (TAPS, 512), 0)
    place = lax.broadcasted_iota(jnp.int32, (TAPS, 512), 1)
    onehot = jnp.where(tap_no + place == TAPS + DEC - 1, 1.0, 0.0).astype(jnp.bfloat16)
    base = jnp.dot(
        jnp.broadcast_to(taps, (64, TAPS)).astype(jnp.bfloat16),
        onehot,
        preferred_element_type=jnp.float32,
    )
    return pltpu.roll(base, 0, 1, stride=DEC, stride_axis=0)


def fir_matrix(rolled, hmat):
    turned = jnp.concatenate([rolled, jnp.zeros_like(rolled)], axis=0).T
    later = pltpu.roll(turned, 64, 1)
    block = jnp.concatenate(
        [turned[:256], turned[256:] + later[:256], later[256:]], axis=0
    ).astype(jnp.bfloat16)
    hmat[0:768, 0:LANE] = block
    hmat[768:, 0:LANE] = jnp.zeros((SPAN - 768, LANE), jnp.bfloat16)
    hmat[0:512, LANE:] = jnp.zeros((512, LANE), jnp.bfloat16)
    hmat[512:, LANE:] = block


def dft_table(band_ref, table, nseg):
    def unit(turn):
        turn = turn & (NFFT - 1)
        quad = ((turn + 128) >> 8) & 3
        rest = ((turn + 128) & 255) - 128
        x = rest.astype(jnp.float32) * (2.0 * math.pi / NFFT)
        x2 = x * x
        sin = x * (1.0 + x2 * (-1.0 / 6 + x2 * (1.0 / 120 + x2 * (-1.0 / 5040 + x2 / 362880))))
        cos = 1.0 + x2 * (
            -0.5 + x2 * (1.0 / 24 + x2 * (-1.0 / 720 + x2 * (1.0 / 40320 - x2 / 3628800)))
        )
        swap = (quad & 1) == 1
        c = jnp.where(swap, sin, cos)
        s = jnp.where(swap, cos, sin)
        c = jnp.where((quad == 1) | (quad == 2), -c, c)
        s = jnp.where(quad >= 2, -s, s)
        return c, s

    lane = lax.broadcasted_iota(jnp.int32, (8, LANE), 1)
    sub = lax.broadcasted_iota(jnp.int32, (8, LANE), 0)
    for b in range(BINS):
        for g in range(0, nseg, 16):
            freq = [band_ref[0] + b + BINS * (sub + g + k) for k in (0, 8)]
            freq = jnp.concatenate(freq, axis=0)
            lanes = jnp.concatenate([lane, lane], axis=0)
            c, s = unit(freq * lanes)
            cr, sr = unit(freq * LANE)
            for a in range(NFFT // LANE):
                at = slice(a * LANE, (a + 1) * LANE)
                table[b * nseg + g : b * nseg + g + 16, at] = c.astype(jnp.bfloat16)
                low = (BINS + b) * nseg + g
                table[low : low + 16, at] = (-s).astype(jnp.bfloat16)
                c, s = c * cr - s * sr, s * cr + c * sr


def products(left, right, factor):
    half = left.shape[0] // 2
    left = left * jnp.bfloat16(factor)
    turned = jnp.concatenate([-left[half:], left[:half]], axis=0)
    return [
        lax.dot_general(
            lhs, right, (((0,), (0,)), ((), ())), preferred_element_type=jnp.float32
        ).astype(jnp.bfloat16)
        for lhs in (left, turned)
    ]


def kernel(
    nseg,
    factor,
    nsrc,
    ndead,
    raw,
    small_ref,
    band_ref,
    done_ref,
    right_last,
    left_last,
    hot,
    xbuf,
    tail,
    trace,
    first,
    hmat,
    table,
    halo_out,
    halo_in,
    spec,
    tiles,
    outbox,
    inbox,
    wide,
    right_ref,
    picked,
    half_in,
    half_sum,
    far_in,
    cross_in,
    total,
    tail_sem,
    raw_sem,
    halo_send,
    halo_recv,
    box_send,
    box_recv,
    ex_send,
    ex_recv,
):
    seg = lax.axis_index("seg")
    chan = lax.axis_index("chan")
    chans = raw.shape[0]
    samples = raw.shape[1]
    core = chan & 1
    sibling = {"chan": chan ^ 1}
    far = {"chan": chan ^ 2}
    cross = {"chan": chan ^ 3}
    nextseg = {"seg": lax.rem(seg + 1, nseg)}

    tail_copy = pltpu.make_async_copy(raw.at[:, pl.ds(samples - TAPS, TAPS)], tail, tail_sem)
    raw_copies = [
        pltpu.make_async_copy(raw.at[pl.ds(c0, w)], xbuf.at[pl.ds(c0, w)], raw_sem.at[q])
        for q, (c0, w) in enumerate(CHUNKS)
    ]
    for copy in (tail_copy, raw_copies[0], raw_copies[1]):
        copy.start()

    barrier = pltpu.get_barrier_semaphore()

    @pl.loop(1, nseg, unroll=7)
    def _(d):
        pl.semaphore_signal(
            barrier, 1, device_id={"seg": lax.rem(seg + d, nseg)}, device_id_type=MESH
        )

    pl.semaphore_signal(barrier, 1, device_id=sibling, device_id_type=MESH)
    pl.semaphore_signal(barrier, 1, device_id=far, device_id_type=MESH)
    pl.semaphore_signal(barrier, 1, device_id=cross, device_id_type=MESH)

    rolled = fir_rows(small_ref[:, :TAPS])
    lane64 = lax.broadcasted_iota(jnp.int32, (1, LANE), 1) < 64
    near = rolled[:, :TAPS]
    low = jnp.concatenate([near, jnp.zeros_like(near)], axis=0).astype(jnp.bfloat16)
    high = jnp.concatenate([jnp.zeros_like(near), near], axis=0).astype(jnp.bfloat16)
    over_time = (((1,), (1,)), ((), ()))
    tail_copy.wait()
    for c0, w in CHUNKS:
        h = w // 2
        part = lax.dot_general(
            tail[c0 : c0 + h], low, over_time, preferred_element_type=jnp.float32
        ) + lax.dot_general(
            tail[c0 + h : c0 + w], high, over_time, preferred_element_type=jnp.float32
        )
        halo_out[c0 // 2 : c0 // 2 + h] = part.astype(jnp.bfloat16)

    pl.semaphore_wait(barrier, nseg + 2)
    halos = []
    for q, (c0, w) in enumerate(CHUNKS):
        rows = pl.ds(c0 // 2, w // 2)
        copy = pltpu.make_async_remote_copy(
            halo_out.at[rows],
            halo_in.at[rows],
            halo_send.at[q],
            halo_recv.at[q],
            device_id=nextseg,
            device_id_type=MESH,
        )
        copy.start()
        halos.append(copy)

    fir_matrix(rolled, hmat)

    def filtered(q):
        c0, w = CHUNKS[q]
        rows = slice(c0, c0 + w)
        raw_copies[q].wait()
        if q + 2 < len(CHUNKS):
            raw_copies[q + 2].start()
        for b in range(NFFT // BLOCK):
            begin = b * DEC * BLOCK - TAPS
            if b == 0:
                acc = jnp.dot(
                    xbuf[rows, 0 : DEC * BLOCK], hmat[TAPS:], preferred_element_type=jnp.float32
                )
                first[rows] = acc[:, :LANE]
                trace[rows, LANE:BLOCK] = acc[:, LANE:].astype(jnp.bfloat16)
            else:
                acc = jnp.dot(
                    xbuf[rows, begin : begin + SPAN], hmat[...], preferred_element_type=jnp.float32
                )
                trace[rows, b * BLOCK : (b + 1) * BLOCK] = acc.astype(jnp.bfloat16)

    filtered(0)
    dft_table(band_ref, table, nseg)

    first_chan = (chan * chans).astype(jnp.float32)
    padded = small_ref[:, TAPS + nsrc :]
    dead = jnp.broadcast_to(padded, (LANE, LANE)).T[:ndead]
    lane = lax.broadcasted_iota(jnp.int32, (1, LANE), 1).astype(jnp.float32)
    alive = []
    for c0 in range(0, chans, LANE):
        hits = jnp.where(dead == lane + (first_chan + (c0 + 1)), 1.0, 0.0)
        alive.append(1.0 - jnp.max(hits, axis=0, keepdims=True))
    has_prior = jnp.where(seg > 0, 1.0, 0.0)
    nothing = jnp.zeros((nseg, LANE), jnp.float32)
    for row in (6, 7, 14, 15):
        tiles[0, pl.ds(row, nseg, stride=ROWS), :] = nothing

    def post(box):
        outbox[box] = tiles[box].reshape(nseg, ROWS, LANE).astype(jnp.bfloat16)
        pltpu.make_async_copy(outbox.at[box, seg], inbox.at[box, seg], box_recv.at[box]).start()

        @pl.loop(1, nseg, unroll=7)
        def _(d):
            to = lax.rem(seg + d, nseg)
            pltpu.make_async_remote_copy(
                outbox.at[box, to],
                inbox.at[box, seg],
                box_send.at[box],
                box_recv.at[box],
                device_id={"seg": to},
                device_id_type=MESH,
            ).start()

    for q, (c0, w) in enumerate(CHUNKS):
        h = w // 2
        halos[q].wait_recv()
        prior = halo_in[c0 // 2 : c0 // 2 + h].astype(jnp.float32) * has_prior
        prior_low = jnp.where(lane64, prior, 0.0)
        prior_high = jnp.where(lane64, pltpu.roll(prior, 64, 1), 0.0)
        trace[c0 : c0 + h, 0:LANE] = (first[c0 : c0 + h] + prior_low).astype(jnp.bfloat16)
        trace[c0 + h : c0 + w, 0:LANE] = (first[c0 + h : c0 + w] + prior_high).astype(jnp.bfloat16)
        spec[:, :w] = lax.dot_general(
            table[...], trace[c0 : c0 + w], over_time, preferred_element_type=jnp.float32
        )
        for at in range(0, w, LANE):
            lanes = slice(at, at + LANE)
            group = (c0 + at) // LANE
            energy = jnp.zeros((8, LANE), jnp.float32)
            for row in range(2 * BINS):
                s = spec[row * nseg : (row + 1) * nseg, lanes].reshape(nseg // 8, 8, LANE)
                energy += jnp.sum(s * s, axis=0)
            level = jnp.sum(energy, axis=0, keepdims=True) * (1.0 / (BINS * nseg))
            live = alive[group]
            for b in range(BINS):
                real = spec[b * nseg : (b + 1) * nseg, lanes]
                imag = spec[(BINS + b) * nseg : (BINS + b + 1) * nseg, lanes]
                gain = live * lax.rsqrt(real * real + imag * imag + (0.1 * level + 1e-6))
                for part, value in enumerate((real, imag)):
                    box, row = box_row(part, b, group)
                    tiles[box, pl.ds(row, nseg, stride=ROWS), :] = value * gain
        if q == 0:
            post(0)
            filtered(1)
        elif q == 1:
            filtered(2)
    for b in range(BINS):
        post(1 + b)

    source = small_ref[:, TAPS : TAPS + nsrc]
    for c0 in range(0, chans, LANE):
        ids = lax.broadcasted_iota(jnp.int32, (LANE, nsrc), 0).astype(jnp.float32)
        hot[c0 : c0 + LANE] = jnp.where(ids + (first_chan + c0) == source, 1.0, 0.0).astype(
            jnp.bfloat16
        )

    def right_of(b):
        return right_last if b == BINS - 1 else right_ref.at[b]

    def collect(box):
        pltpu.make_async_copy(inbox.at[box], inbox.at[box], box_recv.at[box]).wait()
        wide[...] = inbox[box].reshape(nseg * ROWS, LANE).astype(jnp.float32)
        for part in range(2):
            for b in range(BINS):
                for group in range(chans // LANE):
                    held, row = box_row(part, b, group)
                    if held == box:
                        right_of(b)[
                            part * nseg : (part + 1) * nseg, group * LANE : (group + 1) * LANE
                        ] = wide[pl.ds(row, nseg, stride=ROWS), :].astype(jnp.bfloat16)

    copies = {}

    def exchange(step, b, src, dst, to):
        copy = pltpu.make_async_remote_copy(
            src,
            dst,
            ex_send.at[step, b],
            ex_recv.at[step, b],
            device_id=to,
            device_id_type=MESH,
        )
        copy.start()
        copies[step, b] = copy

    def step_pick(b):
        acc = jnp.dot(right_of(b)[...], hot[...], preferred_element_type=jnp.float32)
        acc = acc.astype(jnp.bfloat16)
        picked[b, 0] = acc[:nseg]
        picked[b, 1] = acc[nseg:]
        exchange(0, b, picked.at[b, 1 - core], half_in.at[b], sibling)
        if b == BINS - 1:
            exchange(1, b, picked.at[b, core], far_in.at[b], far)
            exchange(3, b, picked.at[b, 1 - core], cross_in, cross)

    def step_far(b):
        copies[0, b].wait_recv()
        if b == BINS - 1:
            half_sum[b] = picked[b, core] + half_in[b]
            copies[3, b].wait_recv()
            half_sum[b] = half_sum[b] + cross_in[...]
            return
        half_sum[b] = picked[b, core] + half_in[b]
        exchange(1, b, half_sum.at[b], far_in.at[b], far)

    def step_back(b):
        copies[1, b].wait_recv()
        total[b, core] = half_sum[b] + far_in[b]
        exchange(2, b, total.at[b, core], total.at[b, core], sibling)

    def step_product(b):
        copies[2, b].wait_recv()
        left = jnp.concatenate([total[b, 0], total[b, 1]], axis=0)
        if b == BINS - 1:
            left_last[...] = left
            return
        for part, value in enumerate(products(left, right_ref[b], factor)):
            done_ref[b, part] = value

    collect(0)
    collect(1)
    step_pick(0)
    collect(2)
    step_pick(1)
    step_far(0)
    step_far(1)
    collect(3)
    step_pick(2)
    step_back(0)
    step_back(1)
    step_product(0)
    step_far(2)
    step_back(2)
    step_product(1)
    step_product(2)
    for copy in copies.values():
        copy.wait_send()
    for copy in halos:
        copy.wait_send()
    for box in range(outbox.shape[0]):
        sent = outbox.at[box, pl.ds(0, nseg - 1)]
        pltpu.make_async_copy(sent, sent, box_send.at[box]).wait()


def finish_kernel(factor, done_ref, right_ref, left_ref, out_ref, buf, sems):
    last = BINS - 1
    copies = [pltpu.make_async_copy(done_ref, out_ref.at[pl.ds(0, last)], sems.at[2])]
    copies[0].start()
    for part, value in enumerate(products(left_ref[...], right_ref[...], factor)):
        buf[part] = value
        copy = pltpu.make_async_copy(buf.at[part], out_ref.at[last, part], sems.at[part])
        copy.start()
        copies.append(copy)
    for copy in copies:
        copy.wait()


def per_device(nseg, raw, fir_taps, band_lo, source_chan, dead_chan):
    chans = raw.shape[0]
    nsrc = source_chan.shape[0]
    ndead = dead_chan.shape[0]
    factor = 1.0 / math.sqrt(nseg)
    vmem = pl.BlockSpec(memory_space=pltpu.VMEM)
    smem = pl.BlockSpec(memory_space=pltpu.SMEM)
    hbm = pl.BlockSpec(memory_space=pltpu.HBM)
    bf16, f32 = jnp.bfloat16, jnp.float32
    nq = len(CHUNKS)
    nbox = 1 + BINS
    small = (
        jnp.pad(fir_taps, (0, nsrc + LANE)).astype(f32)
        + jnp.pad(source_chan, (TAPS, LANE)).astype(f32)
        + (jnp.pad(dead_chan, (TAPS + nsrc, LANE - ndead), constant_values=-1).astype(f32) + 1.0)
    ).reshape(1, TAPS + nsrc + LANE)
    done, right, left = pl.pallas_call(
        functools.partial(kernel, nseg, factor, nsrc, ndead),
        out_shape=(
            jax.ShapeDtypeStruct((BINS - 1, 2, nsrc, chans), bf16),
            jax.ShapeDtypeStruct((2 * nseg, chans), bf16),
            jax.ShapeDtypeStruct((2 * nseg, nsrc), bf16),
        ),
        in_specs=[hbm, vmem, smem],
        out_specs=(vmem, vmem, vmem),
        scratch_shapes=[
            pltpu.VMEM((chans, nsrc), bf16),
            pltpu.VMEM(raw.shape, bf16),
            pltpu.VMEM((chans, TAPS), bf16),
            pltpu.VMEM((chans, NFFT), bf16),
            pltpu.VMEM((chans, LANE), f32),
            pltpu.VMEM((SPAN, BLOCK), bf16),
            pltpu.VMEM((2 * BINS * nseg, NFFT), bf16),
            pltpu.VMEM((chans // 2, LANE), bf16),
            pltpu.VMEM((chans // 2, LANE), bf16),
            pltpu.VMEM((2 * BINS * nseg, 512), f32),
            pltpu.VMEM((nbox, nseg * ROWS, LANE), f32),
            pltpu.VMEM((nbox, nseg, ROWS, LANE), bf16),
            pltpu.VMEM((nbox, nseg, ROWS, LANE), bf16),
            pltpu.VMEM((nseg * ROWS, LANE), f32),
            pltpu.VMEM((BINS - 1, 2 * nseg, chans), bf16),
            pltpu.VMEM((BINS, 2, nseg, nsrc), bf16),
            pltpu.VMEM((BINS, nseg, nsrc), bf16),
            pltpu.VMEM((BINS, nseg, nsrc), bf16),
            pltpu.VMEM((BINS, nseg, nsrc), bf16),
            pltpu.VMEM((nseg, nsrc), bf16),
            pltpu.VMEM((BINS, 2, nseg, nsrc), bf16),
            pltpu.SemaphoreType.DMA,
            pltpu.SemaphoreType.DMA((nq,)),
            pltpu.SemaphoreType.DMA((nq,)),
            pltpu.SemaphoreType.DMA((nq,)),
            pltpu.SemaphoreType.DMA((nbox,)),
            pltpu.SemaphoreType.DMA((nbox,)),
            pltpu.SemaphoreType.DMA((4, BINS)),
            pltpu.SemaphoreType.DMA((4, BINS)),
        ],
        compiler_params=pltpu.CompilerParams(
            collective_id=0, has_side_effects=True, vmem_limit_bytes=44 * 1024 * 1024
        ),
        name="whiten_exchange",
    )(raw, small, band_lo)
    return pl.pallas_call(
        functools.partial(finish_kernel, factor),
        out_shape=jax.ShapeDtypeStruct((BINS, 2, nsrc, chans), bf16),
        in_specs=[vmem, vmem, vmem],
        out_specs=hbm,
        scratch_shapes=[
            pltpu.VMEM((2, nsrc, chans), bf16),
            pltpu.SemaphoreType.DMA((3,)),
        ],
        compiler_params=pltpu.CompilerParams(vmem_limit_bytes=32 * 1024 * 1024),
        name="finish",
    )(done, right, left)


def solution(mesh):
    return jax.shard_map(
        functools.partial(per_device, mesh.shape["seg"]),
        mesh=mesh,
        in_specs=(P("chan", "seg"), P(), P(), P(), P()),
        out_specs=P("seg", None, None, "chan"),
        check_vma=False,
    )
```

```python
import functools
import math

import jax
import jax.numpy as jnp
from jax import lax
from jax.experimental import pallas as pl
from jax.experimental.pallas import tpu as pltpu
from jax.sharding import PartitionSpec as P

NFFT = 1024
DEC = 4
TAPS = 256
BINS = 3
LANE = 128
BLOCK = 256
SPAN = DEC * BLOCK + TAPS
CHUNKS = ((1024, 256), (0, 512), (512, 512))
ROWS = 16
MESH = pl.DeviceIdType.MESH


def box_row(part, b, group):
    if group < 8:
        return 1 + b, 8 * part + group
    return 0, 8 * part + 2 * b + group - 8


def fir_rows(taps):
    tap_no = lax.broadcasted_iota(jnp.int32, (TAPS, 512), 0)
    place = lax.broadcasted_iota(jnp.int32, (TAPS, 512), 1)
    onehot = jnp.where(tap_no + place == TAPS + DEC - 1, 1.0, 0.0).astype(jnp.bfloat16)
    base = jnp.dot(
        jnp.broadcast_to(taps, (64, TAPS)).astype(jnp.bfloat16),
        onehot,
        preferred_element_type=jnp.float32,
    )
    return pltpu.roll(base, 0, 1, stride=DEC, stride_axis=0)


def fir_matrix(rolled, hmat):
    turned = jnp.concatenate([rolled, jnp.zeros_like(rolled)], axis=0).T
    later = pltpu.roll(turned, 64, 1)
    block = jnp.concatenate(
        [turned[:256], turned[256:] + later[:256], later[256:]], axis=0
    ).astype(jnp.bfloat16)
    hmat[0:768, 0:LANE] = block
    hmat[768:, 0:LANE] = jnp.zeros((SPAN - 768, LANE), jnp.bfloat16)
    hmat[0:512, LANE:] = jnp.zeros((512, LANE), jnp.bfloat16)
    hmat[512:, LANE:] = block


def dft_table(band_ref, table, nseg):
    def unit(turn):
        turn = turn & (NFFT - 1)
        quad = ((turn + 128) >> 8) & 3
        rest = ((turn + 128) & 255) - 128
        x = rest.astype(jnp.float32) * (2.0 * math.pi / NFFT)
        x2 = x * x
        sin = x * (1.0 + x2 * (-1.0 / 6 + x2 * (1.0 / 120 + x2 * (-1.0 / 5040 + x2 / 362880))))
        cos = 1.0 + x2 * (
            -0.5 + x2 * (1.0 / 24 + x2 * (-1.0 / 720 + x2 * (1.0 / 40320 - x2 / 3628800)))
        )
        swap = (quad & 1) == 1
        c = jnp.where(swap, sin, cos)
        s = jnp.where(swap, cos, sin)
        c = jnp.where((quad == 1) | (quad == 2), -c, c)
        s = jnp.where(quad >= 2, -s, s)
        return c, s

    lane = lax.broadcasted_iota(jnp.int32, (8, LANE), 1)
    sub = lax.broadcasted_iota(jnp.int32, (8, LANE), 0)
    for b in range(BINS):
        for g in range(0, nseg, 16):
            freq = [band_ref[0] + b + BINS * (sub + g + k) for k in (0, 8)]
            freq = jnp.concatenate(freq, axis=0)
            lanes = jnp.concatenate([lane, lane], axis=0)
            c, s = unit(freq * lanes)
            cr, sr = unit(freq * LANE)
            for a in range(NFFT // LANE):
                at = slice(a * LANE, (a + 1) * LANE)
                table[b * nseg + g : b * nseg + g + 16, at] = c.astype(jnp.bfloat16)
                low = (BINS + b) * nseg + g
                table[low : low + 16, at] = (-s).astype(jnp.bfloat16)
                c, s = c * cr - s * sr, s * cr + c * sr


def products(left, right, factor):
    half = left.shape[0] // 2
    left = left * jnp.bfloat16(factor)
    turned = jnp.concatenate([-left[half:], left[:half]], axis=0)
    return [
        lax.dot_general(
            lhs, right, (((0,), (0,)), ((), ())), preferred_element_type=jnp.float32
        ).astype(jnp.bfloat16)
        for lhs in (left, turned)
    ]


def kernel(
    nseg,
    factor,
    nsrc,
    ndead,
    raw,
    small_ref,
    band_ref,
    done_ref,
    right_last,
    left_last,
    hot,
    xbuf,
    tail,
    trace,
    first,
    hmat,
    table,
    halo_out,
    halo_in,
    spec,
    tiles,
    outbox,
    inbox,
    wide,
    right_ref,
    picked,
    half_in,
    half_sum,
    far_in,
    cross_in,
    total,
    tail_sem,
    raw_sem,
    halo_send,
    halo_recv,
    box_send,
    box_recv,
    ex_send,
    ex_recv,
):
    seg = lax.axis_index("seg")
    chan = lax.axis_index("chan")
    chans = raw.shape[0]
    samples = raw.shape[1]
    core = chan & 1
    sibling = {"chan": chan ^ 1}
    far = {"chan": chan ^ 2}
    cross = {"chan": chan ^ 3}
    nextseg = {"seg": lax.rem(seg + 1, nseg)}

    tail_copy = pltpu.make_async_copy(raw.at[:, pl.ds(samples - TAPS, TAPS)], tail, tail_sem)
    raw_copies = [
        pltpu.make_async_copy(raw.at[pl.ds(c0, w)], xbuf.at[pl.ds(c0, w)], raw_sem.at[q])
        for q, (c0, w) in enumerate(CHUNKS)
    ]
    for copy in (tail_copy, raw_copies[0], raw_copies[1]):
        copy.start()

    barrier = pltpu.get_barrier_semaphore()

    pl.semaphore_signal(barrier, 1, device_id=sibling, device_id_type=MESH)
    pl.semaphore_signal(barrier, 1, device_id=far, device_id_type=MESH)
    pl.semaphore_signal(barrier, 1, device_id=cross, device_id_type=MESH)

    @pl.loop(1, nseg, unroll=21)
    def _(d):
        pl.semaphore_signal(
            barrier, 1, device_id={"seg": seg ^ (nseg - d)}, device_id_type=MESH
        )


    rolled = fir_rows(small_ref[:, :TAPS])
    lane64 = lax.broadcasted_iota(jnp.int32, (1, LANE), 1) < 64
    near = rolled[:, :TAPS]
    low = jnp.concatenate([near, jnp.zeros_like(near)], axis=0).astype(jnp.bfloat16)
    high = jnp.concatenate([jnp.zeros_like(near), near], axis=0).astype(jnp.bfloat16)
    over_time = (((1,), (1,)), ((), ()))
    tail_copy.wait()
    for c0, w in CHUNKS:
        h = w // 2
        part = lax.dot_general(
            tail[c0 : c0 + h], low, over_time, preferred_element_type=jnp.float32
        ) + lax.dot_general(
            tail[c0 + h : c0 + w], high, over_time, preferred_element_type=jnp.float32
        )
        halo_out[c0 // 2 : c0 // 2 + h] = part.astype(jnp.bfloat16)

    pl.semaphore_wait(barrier, nseg + 2)
    halos = []
    for q, (c0, w) in enumerate(CHUNKS):
        rows = pl.ds(c0 // 2, w // 2)
        copy = pltpu.make_async_remote_copy(
            halo_out.at[rows],
            halo_in.at[rows],
            halo_send.at[q],
            halo_recv.at[q],
            device_id=nextseg,
            device_id_type=MESH,
        )
        copy.start()
        halos.append(copy)

    fir_matrix(rolled, hmat)

    def filtered(q):
        c0, w = CHUNKS[q]
        rows = slice(c0, c0 + w)
        raw_copies[q].wait()
        if q + 2 < len(CHUNKS):
            raw_copies[q + 2].start()
        for b in range(NFFT // BLOCK):
            begin = b * DEC * BLOCK - TAPS
            if b == 0:
                acc = jnp.dot(
                    xbuf[rows, 0 : DEC * BLOCK], hmat[TAPS:], preferred_element_type=jnp.float32
                )
                first[rows] = acc[:, :LANE]
                trace[rows, LANE:BLOCK] = acc[:, LANE:].astype(jnp.bfloat16)
            else:
                acc = jnp.dot(
                    xbuf[rows, begin : begin + SPAN], hmat[...], preferred_element_type=jnp.float32
                )
                trace[rows, b * BLOCK : (b + 1) * BLOCK] = acc.astype(jnp.bfloat16)

    filtered(0)
    dft_table(band_ref, table, nseg)

    first_chan = (chan * chans).astype(jnp.float32)
    padded = small_ref[:, TAPS + nsrc :]
    dead = jnp.broadcast_to(padded, (LANE, LANE)).T[:ndead]
    lane = lax.broadcasted_iota(jnp.int32, (1, LANE), 1).astype(jnp.float32)
    alive = []
    for c0 in range(0, chans, LANE):
        hits = jnp.where(dead == lane + (first_chan + (c0 + 1)), 1.0, 0.0)
        alive.append(1.0 - jnp.max(hits, axis=0, keepdims=True))
    has_prior = jnp.where(seg > 0, 1.0, 0.0)
    nothing = jnp.zeros((nseg, LANE), jnp.float32)
    for row in (6, 7, 14, 15):
        tiles[0, pl.ds(row, nseg, stride=ROWS), :] = nothing

    def post(box):
        outbox[box] = tiles[box].reshape(nseg, ROWS, LANE).astype(jnp.bfloat16)
        pltpu.make_async_copy(outbox.at[box, seg], inbox.at[box, seg], box_recv.at[box]).start()

        @pl.loop(1, nseg, unroll=21)
        def _(d):
            to = lax.rem(seg + d, nseg)
            pltpu.make_async_remote_copy(
                outbox.at[box, to],
                inbox.at[box, seg],
                box_send.at[box],
                box_recv.at[box],
                device_id={"seg": to},
                device_id_type=MESH,
            ).start()

    for q, (c0, w) in enumerate(CHUNKS):
        h = w // 2
        halos[q].wait_recv()
        prior = halo_in[c0 // 2 : c0 // 2 + h].astype(jnp.float32) * has_prior
        prior_low = jnp.where(lane64, prior, 0.0)
        prior_high = jnp.where(lane64, pltpu.roll(prior, 64, 1), 0.0)
        trace[c0 : c0 + h, 0:LANE] = (first[c0 : c0 + h] + prior_low).astype(jnp.bfloat16)
        trace[c0 + h : c0 + w, 0:LANE] = (first[c0 + h : c0 + w] + prior_high).astype(jnp.bfloat16)
        spec[:, :w] = lax.dot_general(
            table[...], trace[c0 : c0 + w], over_time, preferred_element_type=jnp.float32
        )
        for at in range(0, w, LANE):
            lanes = slice(at, at + LANE)
            group = (c0 + at) // LANE
            energy = jnp.zeros((8, LANE), jnp.float32)
            for row in range(2 * BINS):
                s = spec[row * nseg : (row + 1) * nseg, lanes].reshape(nseg // 8, 8, LANE)
                energy += jnp.sum(s * s, axis=0)
            level = jnp.sum(energy, axis=0, keepdims=True) * (1.0 / (BINS * nseg))
            live = alive[group]
            for b in range(BINS):
                real = spec[b * nseg : (b + 1) * nseg, lanes]
                imag = spec[(BINS + b) * nseg : (BINS + b + 1) * nseg, lanes]
                gain = live * lax.rsqrt(real * real + imag * imag + (0.1 * level + 1e-6))
                for part, value in enumerate((real, imag)):
                    box, row = box_row(part, b, group)
                    tiles[box, pl.ds(row, nseg, stride=ROWS), :] = value * gain
        if q == 0:
            post(0)
            filtered(1)
        elif q == 1:
            filtered(2)
    for b in range(BINS):
        post(1 + b)

    source = small_ref[:, TAPS : TAPS + nsrc]
    for c0 in range(0, chans, LANE):
        ids = lax.broadcasted_iota(jnp.int32, (LANE, nsrc), 0).astype(jnp.float32)
        hot[c0 : c0 + LANE] = jnp.where(ids + (first_chan + c0) == source, 1.0, 0.0).astype(
            jnp.bfloat16
        )

    def right_of(b):
        return right_last if b == BINS - 1 else right_ref.at[b]

    def collect(box):
        pltpu.make_async_copy(inbox.at[box], inbox.at[box], box_recv.at[box]).wait()
        wide[...] = inbox[box].reshape(nseg * ROWS, LANE).astype(jnp.float32)
        for part in range(2):
            for b in range(BINS):
                for group in range(chans // LANE):
                    held, row = box_row(part, b, group)
                    if held == box:
                        right_of(b)[
                            part * nseg : (part + 1) * nseg, group * LANE : (group + 1) * LANE
                        ] = wide[pl.ds(row, nseg, stride=ROWS), :].astype(jnp.bfloat16)

    copies = {}

    def exchange(step, b, src, dst, to):
        copy = pltpu.make_async_remote_copy(
            src,
            dst,
            ex_send.at[step, b],
            ex_recv.at[step, b],
            device_id=to,
            device_id_type=MESH,
        )
        copy.start()
        copies[step, b] = copy

    def step_pick(b):
        acc = jnp.dot(right_of(b)[...], hot[...], preferred_element_type=jnp.float32)
        acc = acc.astype(jnp.bfloat16)
        picked[b, 0] = acc[:nseg]
        picked[b, 1] = acc[nseg:]
        exchange(0, b, picked.at[b, 1 - core], half_in.at[b], sibling)
        if b == BINS - 1:
            exchange(1, b, picked.at[b, core], far_in.at[b], far)
            exchange(3, b, picked.at[b, 1 - core], cross_in, cross)

    def step_far(b):
        copies[0, b].wait_recv()
        if b == BINS - 1:
            half_sum[b] = picked[b, core] + half_in[b]
            copies[3, b].wait_recv()
            half_sum[b] = half_sum[b] + cross_in[...]
            return
        half_sum[b] = picked[b, core] + half_in[b]
        exchange(1, b, half_sum.at[b], far_in.at[b], far)

    def step_back(b):
        copies[1, b].wait_recv()
        total[b, core] = half_sum[b] + far_in[b]
        exchange(2, b, total.at[b, core], total.at[b, core], sibling)

    def step_product(b):
        copies[2, b].wait_recv()
        left = jnp.concatenate([total[b, 0], total[b, 1]], axis=0)
        if b == BINS - 1:
            left_last[...] = left
            return
        for part, value in enumerate(products(left, right_ref[b], factor)):
            done_ref[b, part] = value

    collect(0)
    collect(1)
    step_pick(0)
    collect(2)
    step_pick(1)
    step_far(0)
    step_far(1)
    collect(3)
    step_pick(2)
    step_back(0)
    step_back(1)
    step_product(0)
    step_far(2)
    step_back(2)
    step_product(1)
    step_product(2)
    for copy in copies.values():
        copy.wait_send()
    for copy in halos:
        copy.wait_send()
    for box in range(outbox.shape[0]):
        sent = outbox.at[box, pl.ds(0, nseg - 1)]
        pltpu.make_async_copy(sent, sent, box_send.at[box]).wait()


def finish_kernel(factor, done_ref, right_ref, left_ref, out_ref, buf, sems):
    last = BINS - 1
    copies = [pltpu.make_async_copy(done_ref, out_ref.at[pl.ds(0, last)], sems.at[2])]
    copies[0].start()
    for part, value in enumerate(products(left_ref[...], right_ref[...], factor)):
        buf[part] = value
        copy = pltpu.make_async_copy(buf.at[part], out_ref.at[last, part], sems.at[part])
        copy.start()
        copies.append(copy)
    for copy in copies:
        copy.wait()


def per_device(nseg, raw, fir_taps, band_lo, source_chan, dead_chan):
    chans = raw.shape[0]
    nsrc = source_chan.shape[0]
    ndead = dead_chan.shape[0]
    factor = 1.0 / math.sqrt(nseg)
    vmem = pl.BlockSpec(memory_space=pltpu.VMEM)
    smem = pl.BlockSpec(memory_space=pltpu.SMEM)
    hbm = pl.BlockSpec(memory_space=pltpu.HBM)
    bf16, f32 = jnp.bfloat16, jnp.float32
    nq = len(CHUNKS)
    nbox = 1 + BINS
    small = (
        jnp.pad(fir_taps, (0, nsrc + LANE)).astype(f32)
        + jnp.pad(source_chan, (TAPS, LANE)).astype(f32)
        + (jnp.pad(dead_chan, (TAPS + nsrc, LANE - ndead), constant_values=-1).astype(f32) + 1.0)
    ).reshape(1, TAPS + nsrc + LANE)
    done, right, left = pl.pallas_call(
        functools.partial(kernel, nseg, factor, nsrc, ndead),
        out_shape=(
            jax.ShapeDtypeStruct((BINS - 1, 2, nsrc, chans), bf16),
            jax.ShapeDtypeStruct((2 * nseg, chans), bf16),
            jax.ShapeDtypeStruct((2 * nseg, nsrc), bf16),
        ),
        in_specs=[hbm, vmem, smem],
        out_specs=(vmem, vmem, vmem),
        scratch_shapes=[
            pltpu.VMEM((chans, nsrc), bf16),
            pltpu.VMEM(raw.shape, bf16),
            pltpu.VMEM((chans, TAPS), bf16),
            pltpu.VMEM((chans, NFFT), bf16),
            pltpu.VMEM((chans, LANE), f32),
            pltpu.VMEM((SPAN, BLOCK), bf16),
            pltpu.VMEM((2 * BINS * nseg, NFFT), bf16),
            pltpu.VMEM((chans // 2, LANE), bf16),
            pltpu.VMEM((chans // 2, LANE), bf16),
            pltpu.VMEM((2 * BINS * nseg, 512), f32),
            pltpu.VMEM((nbox, nseg * ROWS, LANE), f32),
            pltpu.VMEM((nbox, nseg, ROWS, LANE), bf16),
            pltpu.VMEM((nbox, nseg, ROWS, LANE), bf16),
            pltpu.VMEM((nseg * ROWS, LANE), f32),
            pltpu.VMEM((BINS - 1, 2 * nseg, chans), bf16),
            pltpu.VMEM((BINS, 2, nseg, nsrc), bf16),
            pltpu.VMEM((BINS, nseg, nsrc), bf16),
            pltpu.VMEM((BINS, nseg, nsrc), bf16),
            pltpu.VMEM((BINS, nseg, nsrc), bf16),
            pltpu.VMEM((nseg, nsrc), bf16),
            pltpu.VMEM((BINS, 2, nseg, nsrc), bf16),
            pltpu.SemaphoreType.DMA,
            pltpu.SemaphoreType.DMA((nq,)),
            pltpu.SemaphoreType.DMA((nq,)),
            pltpu.SemaphoreType.DMA((nq,)),
            pltpu.SemaphoreType.DMA((nbox,)),
            pltpu.SemaphoreType.DMA((nbox,)),
            pltpu.SemaphoreType.DMA((4, BINS)),
            pltpu.SemaphoreType.DMA((4, BINS)),
        ],
        compiler_params=pltpu.CompilerParams(
            collective_id=0, has_side_effects=True, vmem_limit_bytes=44 * 1024 * 1024
        ),
        name="whiten_exchange",
    )(raw, small, band_lo)
    return pl.pallas_call(
        functools.partial(finish_kernel, factor),
        out_shape=jax.ShapeDtypeStruct((BINS, 2, nsrc, chans), bf16),
        in_specs=[vmem, vmem, vmem],
        out_specs=hbm,
        scratch_shapes=[
            pltpu.VMEM((2, nsrc, chans), bf16),
            pltpu.SemaphoreType.DMA((3,)),
        ],
        compiler_params=pltpu.CompilerParams(vmem_limit_bytes=32 * 1024 * 1024),
        name="finish",
    )(done, right, left)


def solution(mesh):
    return jax.shard_map(
        functools.partial(per_device, mesh.shape["seg"]),
        mesh=mesh,
        in_specs=(P("chan", "seg"), P(), P(), P(), P()),
        out_specs=P("seg", None, None, "chan"),
        check_vma=False,
    )
```

```python
import functools
import math

import jax
import jax.numpy as jnp
from jax import lax
from jax.experimental import pallas as pl
from jax.experimental.pallas import tpu as pltpu
from jax.sharding import PartitionSpec as P

NFFT = 1024
DEC = 4
TAPS = 256
BINS = 3
LANE = 128
BLOCK = 256
SPAN = DEC * BLOCK + TAPS
CHUNKS = ((1024, 256), (0, 512), (512, 512))
ROWS = 16
MESH = pl.DeviceIdType.MESH


def box_row(part, b, group):
    if group < 8:
        return 1 + b, 8 * part + group
    return 0, 8 * part + 2 * b + group - 8


def fir_rows(taps):
    tap_no = lax.broadcasted_iota(jnp.int32, (TAPS, 512), 0)
    place = lax.broadcasted_iota(jnp.int32, (TAPS, 512), 1)
    onehot = jnp.where(tap_no + place == TAPS + DEC - 1, 1.0, 0.0).astype(jnp.bfloat16)
    base = jnp.dot(
        jnp.broadcast_to(taps, (64, TAPS)).astype(jnp.bfloat16),
        onehot,
        preferred_element_type=jnp.float32,
    )
    return pltpu.roll(base, 0, 1, stride=DEC, stride_axis=0)


def fir_matrix(rolled, hmat):
    turned = jnp.concatenate([rolled, jnp.zeros_like(rolled)], axis=0).T
    later = pltpu.roll(turned, 64, 1)
    block = jnp.concatenate(
        [turned[:256], turned[256:] + later[:256], later[256:]], axis=0
    ).astype(jnp.bfloat16)
    hmat[0:768, 0:LANE] = block
    hmat[768:, 0:LANE] = jnp.zeros((SPAN - 768, LANE), jnp.bfloat16)
    hmat[0:512, LANE:] = jnp.zeros((512, LANE), jnp.bfloat16)
    hmat[512:, LANE:] = block


def dft_table(band_ref, table, nseg):
    def unit(turn):
        turn = turn & (NFFT - 1)
        quad = ((turn + 128) >> 8) & 3
        rest = ((turn + 128) & 255) - 128
        x = rest.astype(jnp.float32) * (2.0 * math.pi / NFFT)
        x2 = x * x
        sin = x * (1.0 + x2 * (-1.0 / 6 + x2 * (1.0 / 120 + x2 * (-1.0 / 5040 + x2 / 362880))))
        cos = 1.0 + x2 * (
            -0.5 + x2 * (1.0 / 24 + x2 * (-1.0 / 720 + x2 * (1.0 / 40320 - x2 / 3628800)))
        )
        swap = (quad & 1) == 1
        c = jnp.where(swap, sin, cos)
        s = jnp.where(swap, cos, sin)
        c = jnp.where((quad == 1) | (quad == 2), -c, c)
        s = jnp.where(quad >= 2, -s, s)
        return c, s

    lane = lax.broadcasted_iota(jnp.int32, (8, LANE), 1)
    sub = lax.broadcasted_iota(jnp.int32, (8, LANE), 0)
    for b in range(BINS):
        for g in range(0, nseg, 16):
            freq = [band_ref[0] + b + BINS * (sub + g + k) for k in (0, 8)]
            freq = jnp.concatenate(freq, axis=0)
            lanes = jnp.concatenate([lane, lane], axis=0)
            c, s = unit(freq * lanes)
            cr, sr = unit(freq * LANE)
            for a in range(NFFT // LANE):
                at = slice(a * LANE, (a + 1) * LANE)
                table[b * nseg + g : b * nseg + g + 16, at] = c.astype(jnp.bfloat16)
                low = (BINS + b) * nseg + g
                table[low : low + 16, at] = (-s).astype(jnp.bfloat16)
                c, s = c * cr - s * sr, s * cr + c * sr


def products(left, right, factor):
    half = left.shape[0] // 2
    left = left * jnp.bfloat16(factor)
    turned = jnp.concatenate([-left[half:], left[:half]], axis=0)
    return [
        lax.dot_general(
            lhs, right, (((0,), (0,)), ((), ())), preferred_element_type=jnp.float32
        ).astype(jnp.bfloat16)
        for lhs in (left, turned)
    ]


def kernel(
    nseg,
    factor,
    nsrc,
    ndead,
    raw,
    small_ref,
    band_ref,
    done_ref,
    right_last,
    left_last,
    hot,
    xbuf,
    tail,
    trace,
    first,
    hmat,
    table,
    halo_out,
    halo_in,
    spec,
    tiles,
    outbox,
    inbox,
    wide,
    right_ref,
    picked,
    half_in,
    half_sum,
    far_in,
    cross_in,
    total,
    tail_sem,
    raw_sem,
    halo_send,
    halo_recv,
    box_send,
    box_recv,
    ex_send,
    ex_recv,
):
    seg = lax.axis_index("seg")
    chan = lax.axis_index("chan")
    chans = raw.shape[0]
    samples = raw.shape[1]
    core = chan & 1
    sibling = {"chan": chan ^ 1}
    far = {"chan": chan ^ 2}
    cross = {"chan": chan ^ 3}
    nextseg = {"seg": lax.rem(seg + 1, nseg)}

    tail_copy = pltpu.make_async_copy(raw.at[:, pl.ds(samples - TAPS, TAPS)], tail, tail_sem)
    raw_copies = [
        pltpu.make_async_copy(raw.at[pl.ds(c0, w)], xbuf.at[pl.ds(c0, w)], raw_sem.at[q])
        for q, (c0, w) in enumerate(CHUNKS)
    ]
    for copy in (tail_copy, raw_copies[0], raw_copies[1]):
        copy.start()

    barrier = pltpu.get_barrier_semaphore()

    pl.semaphore_signal(barrier, 1, device_id=sibling, device_id_type=MESH)
    pl.semaphore_signal(barrier, 1, device_id=far, device_id_type=MESH)
    pl.semaphore_signal(barrier, 1, device_id=cross, device_id_type=MESH)

    @pl.loop(1, nseg, unroll=21)
    def _(d):
        pl.semaphore_signal(
            barrier, 1, device_id={"seg": seg ^ (nseg - d)}, device_id_type=MESH
        )


    rolled = fir_rows(small_ref[:, :TAPS])
    lane64 = lax.broadcasted_iota(jnp.int32, (1, LANE), 1) < 64
    near = rolled[:, :TAPS]
    low = jnp.concatenate([near, jnp.zeros_like(near)], axis=0).astype(jnp.bfloat16)
    high = jnp.concatenate([jnp.zeros_like(near), near], axis=0).astype(jnp.bfloat16)
    over_time = (((1,), (1,)), ((), ()))
    tail_copy.wait()
    for c0, w in CHUNKS:
        h = w // 2
        part = lax.dot_general(
            tail[c0 : c0 + h], low, over_time, preferred_element_type=jnp.float32
        ) + lax.dot_general(
            tail[c0 + h : c0 + w], high, over_time, preferred_element_type=jnp.float32
        )
        halo_out[c0 // 2 : c0 // 2 + h] = part.astype(jnp.bfloat16)

    pl.semaphore_wait(barrier, nseg + 2)
    halos = []
    for q, (c0, w) in enumerate(CHUNKS):
        rows = pl.ds(c0 // 2, w // 2)
        copy = pltpu.make_async_remote_copy(
            halo_out.at[rows],
            halo_in.at[rows],
            halo_send.at[q],
            halo_recv.at[q],
            device_id=nextseg,
            device_id_type=MESH,
        )
        copy.start()
        halos.append(copy)

    fir_matrix(rolled, hmat)

    def filtered(q):
        c0, w = CHUNKS[q]
        rows = slice(c0, c0 + w)
        raw_copies[q].wait()
        if q + 2 < len(CHUNKS):
            raw_copies[q + 2].start()
        for b in range(NFFT // BLOCK):
            begin = b * DEC * BLOCK - TAPS
            if b == 0:
                acc = jnp.dot(
                    xbuf[rows, 0 : DEC * BLOCK], hmat[TAPS:], preferred_element_type=jnp.float32
                )
                first[rows] = acc[:, :LANE]
                trace[rows, LANE:BLOCK] = acc[:, LANE:].astype(jnp.bfloat16)
            else:
                acc = jnp.dot(
                    xbuf[rows, begin : begin + SPAN], hmat[...], preferred_element_type=jnp.float32
                )
                trace[rows, b * BLOCK : (b + 1) * BLOCK] = acc.astype(jnp.bfloat16)

    filtered(0)
    dft_table(band_ref, table, nseg)

    first_chan = (chan * chans).astype(jnp.float32)
    padded = small_ref[:, TAPS + nsrc :]
    dead = jnp.broadcast_to(padded, (LANE, LANE)).T[:ndead]
    lane = lax.broadcasted_iota(jnp.int32, (1, LANE), 1).astype(jnp.float32)
    alive = []
    for c0 in range(0, chans, LANE):
        hits = jnp.where(dead == lane + (first_chan + (c0 + 1)), 1.0, 0.0)
        alive.append(1.0 - jnp.max(hits, axis=0, keepdims=True))
    has_prior = jnp.where(seg > 0, 1.0, 0.0)
    nothing = jnp.zeros((nseg, LANE), jnp.float32)
    for row in (6, 7, 14, 15):
        tiles[0, pl.ds(row, nseg, stride=ROWS), :] = nothing

    def post(box):
        outbox[box] = tiles[box].reshape(nseg, ROWS, LANE).astype(jnp.bfloat16)
        pltpu.make_async_copy(outbox.at[box, seg], inbox.at[box, seg], box_recv.at[box]).start()

        @pl.loop(1, nseg, unroll=21)
        def _(d):
            to = lax.rem(seg + d, nseg)
            pltpu.make_async_remote_copy(
                outbox.at[box, to],
                inbox.at[box, seg],
                box_send.at[box],
                box_recv.at[box],
                device_id={"seg": to},
                device_id_type=MESH,
            ).start()

    for q, (c0, w) in enumerate(CHUNKS):
        h = w // 2
        halos[q].wait_recv()
        prior = halo_in[c0 // 2 : c0 // 2 + h].astype(jnp.float32) * has_prior
        prior_low = jnp.where(lane64, prior, 0.0)
        prior_high = jnp.where(lane64, pltpu.roll(prior, 64, 1), 0.0)
        trace[c0 : c0 + h, 0:LANE] = (first[c0 : c0 + h] + prior_low).astype(jnp.bfloat16)
        trace[c0 + h : c0 + w, 0:LANE] = (first[c0 + h : c0 + w] + prior_high).astype(jnp.bfloat16)
        spec[:, :w] = lax.dot_general(
            table[...], trace[c0 : c0 + w], over_time, preferred_element_type=jnp.float32
        )
        for at in range(0, w, LANE):
            lanes = slice(at, at + LANE)
            group = (c0 + at) // LANE
            energy = jnp.zeros((8, LANE), jnp.float32)
            for row in range(2 * BINS):
                s = spec[row * nseg : (row + 1) * nseg, lanes].reshape(nseg // 8, 8, LANE)
                energy += jnp.sum(s * s, axis=0)
            level = jnp.sum(energy, axis=0, keepdims=True) * (1.0 / (BINS * nseg))
            live = alive[group]
            for b in range(BINS):
                real = spec[b * nseg : (b + 1) * nseg, lanes]
                imag = spec[(BINS + b) * nseg : (BINS + b + 1) * nseg, lanes]
                gain = live * lax.rsqrt(real * real + imag * imag + (0.1 * level + 1e-6))
                for part, value in enumerate((real, imag)):
                    box, row = box_row(part, b, group)
                    tiles[box, pl.ds(row, nseg, stride=ROWS), :] = value * gain
        if q == 0:
            post(0)
            filtered(1)
        elif q == 1:
            filtered(2)
    for b in range(BINS):
        post(1 + b)

    source = small_ref[:, TAPS : TAPS + nsrc]
    for c0 in range(0, chans, LANE):
        ids = lax.broadcasted_iota(jnp.int32, (LANE, nsrc), 0).astype(jnp.float32)
        hot[c0 : c0 + LANE] = jnp.where(ids + (first_chan + c0) == source, 1.0, 0.0).astype(
            jnp.bfloat16
        )

    def right_of(b):
        return right_last if b == BINS - 1 else right_ref.at[b]

    def collect(box):
        pltpu.make_async_copy(inbox.at[box], inbox.at[box], box_recv.at[box]).wait()
        wide[...] = inbox[box].reshape(nseg * ROWS, LANE).astype(jnp.float32)
        for part in range(2):
            for b in range(BINS):
                for group in range(chans // LANE):
                    held, row = box_row(part, b, group)
                    if held == box:
                        right_of(b)[
                            part * nseg : (part + 1) * nseg, group * LANE : (group + 1) * LANE
                        ] = wide[pl.ds(row, nseg, stride=ROWS), :].astype(jnp.bfloat16)

    copies = {}

    def exchange(step, b, src, dst, to):
        copy = pltpu.make_async_remote_copy(
            src,
            dst,
            ex_send.at[step, b],
            ex_recv.at[step, b],
            device_id=to,
            device_id_type=MESH,
        )
        copy.start()
        copies[step, b] = copy

    def step_pick(b):
        if b == BINS - 1:
            acc = early + jnp.dot(
                right_last[:, :1024], hot[:1024], preferred_element_type=jnp.float32
            )
        else:
            acc = jnp.dot(right_of(b)[...], hot[...], preferred_element_type=jnp.float32)
        acc = acc.astype(jnp.bfloat16)
        picked[b, 0] = acc[:nseg]
        picked[b, 1] = acc[nseg:]
        exchange(0, b, picked.at[b, 1 - core], half_in.at[b], sibling)
        if b == BINS - 1:
            exchange(1, b, picked.at[b, core], far_in.at[b], far)
            exchange(3, b, picked.at[b, 1 - core], cross_in, cross)

    def step_far(b):
        copies[0, b].wait_recv()
        if b == BINS - 1:
            half_sum[b] = picked[b, core] + half_in[b]
            copies[3, b].wait_recv()
            half_sum[b] = half_sum[b] + cross_in[...]
            return
        half_sum[b] = picked[b, core] + half_in[b]
        exchange(1, b, half_sum.at[b], far_in.at[b], far)

    def step_back(b):
        copies[1, b].wait_recv()
        total[b, core] = half_sum[b] + far_in[b]
        exchange(2, b, total.at[b, core], total.at[b, core], sibling)

    def step_product(b):
        copies[2, b].wait_recv()
        left = jnp.concatenate([total[b, 0], total[b, 1]], axis=0)
        if b == BINS - 1:
            left_last[...] = left
            return
        for part, value in enumerate(products(left, right_ref[b], factor)):
            done_ref[b, part] = value

    collect(0)
    early = jnp.dot(right_last[:, 1024:], hot[1024:], preferred_element_type=jnp.float32)
    collect(1)
    step_pick(0)
    collect(2)
    step_pick(1)
    step_far(0)
    step_far(1)
    collect(3)
    step_pick(2)
    step_back(0)
    step_back(1)
    step_product(0)
    step_far(2)
    step_back(2)
    step_product(1)
    step_product(2)
    for copy in copies.values():
        copy.wait_send()
    for copy in halos:
        copy.wait_send()
    for box in range(outbox.shape[0]):
        sent = outbox.at[box, pl.ds(0, nseg - 1)]
        pltpu.make_async_copy(sent, sent, box_send.at[box]).wait()


def finish_kernel(factor, done_ref, right_ref, left_ref, out_ref, buf, sems):
    last = BINS - 1
    copies = [pltpu.make_async_copy(done_ref, out_ref.at[pl.ds(0, last)], sems.at[2])]
    copies[0].start()
    for part, value in enumerate(products(left_ref[...], right_ref[...], factor)):
        buf[part] = value
        copy = pltpu.make_async_copy(buf.at[part], out_ref.at[last, part], sems.at[part])
        copy.start()
        copies.append(copy)
    for copy in copies:
        copy.wait()


def per_device(nseg, raw, fir_taps, band_lo, source_chan, dead_chan):
    chans = raw.shape[0]
    nsrc = source_chan.shape[0]
    ndead = dead_chan.shape[0]
    factor = 1.0 / math.sqrt(nseg)
    vmem = pl.BlockSpec(memory_space=pltpu.VMEM)
    smem = pl.BlockSpec(memory_space=pltpu.SMEM)
    hbm = pl.BlockSpec(memory_space=pltpu.HBM)
    bf16, f32 = jnp.bfloat16, jnp.float32
    nq = len(CHUNKS)
    nbox = 1 + BINS
    small = (
        jnp.pad(fir_taps, (0, nsrc + LANE)).astype(f32)
        + jnp.pad(source_chan, (TAPS, LANE)).astype(f32)
        + (jnp.pad(dead_chan, (TAPS + nsrc, LANE - ndead), constant_values=-1).astype(f32) + 1.0)
    ).reshape(1, TAPS + nsrc + LANE)
    done, right, left = pl.pallas_call(
        functools.partial(kernel, nseg, factor, nsrc, ndead),
        out_shape=(
            jax.ShapeDtypeStruct((BINS - 1, 2, nsrc, chans), bf16),
            jax.ShapeDtypeStruct((2 * nseg, chans), bf16),
            jax.ShapeDtypeStruct((2 * nseg, nsrc), bf16),
        ),
        in_specs=[hbm, vmem, smem],
        out_specs=(vmem, vmem, vmem),
        scratch_shapes=[
            pltpu.VMEM((chans, nsrc), bf16),
            pltpu.VMEM(raw.shape, bf16),
            pltpu.VMEM((chans, TAPS), bf16),
            pltpu.VMEM((chans, NFFT), bf16),
            pltpu.VMEM((chans, LANE), f32),
            pltpu.VMEM((SPAN, BLOCK), bf16),
            pltpu.VMEM((2 * BINS * nseg, NFFT), bf16),
            pltpu.VMEM((chans // 2, LANE), bf16),
            pltpu.VMEM((chans // 2, LANE), bf16),
            pltpu.VMEM((2 * BINS * nseg, 512), f32),
            pltpu.VMEM((nbox, nseg * ROWS, LANE), f32),
            pltpu.VMEM((nbox, nseg, ROWS, LANE), bf16),
            pltpu.VMEM((nbox, nseg, ROWS, LANE), bf16),
            pltpu.VMEM((nseg * ROWS, LANE), f32),
            pltpu.VMEM((BINS - 1, 2 * nseg, chans), bf16),
            pltpu.VMEM((BINS, 2, nseg, nsrc), bf16),
            pltpu.VMEM((BINS, nseg, nsrc), bf16),
            pltpu.VMEM((BINS, nseg, nsrc), bf16),
            pltpu.VMEM((BINS, nseg, nsrc), bf16),
            pltpu.VMEM((nseg, nsrc), bf16),
            pltpu.VMEM((BINS, 2, nseg, nsrc), bf16),
            pltpu.SemaphoreType.DMA,
            pltpu.SemaphoreType.DMA((nq,)),
            pltpu.SemaphoreType.DMA((nq,)),
            pltpu.SemaphoreType.DMA((nq,)),
            pltpu.SemaphoreType.DMA((nbox,)),
            pltpu.SemaphoreType.DMA((nbox,)),
            pltpu.SemaphoreType.DMA((4, BINS)),
            pltpu.SemaphoreType.DMA((4, BINS)),
        ],
        compiler_params=pltpu.CompilerParams(
            collective_id=0, has_side_effects=True, vmem_limit_bytes=44 * 1024 * 1024
        ),
        name="whiten_exchange",
    )(raw, small, band_lo)
    return pl.pallas_call(
        functools.partial(finish_kernel, factor),
        out_shape=jax.ShapeDtypeStruct((BINS, 2, nsrc, chans), bf16),
        in_specs=[vmem, vmem, vmem],
        out_specs=hbm,
        scratch_shapes=[
            pltpu.VMEM((2, nsrc, chans), bf16),
            pltpu.SemaphoreType.DMA((3,)),
        ],
        compiler_params=pltpu.CompilerParams(vmem_limit_bytes=32 * 1024 * 1024),
        name="finish",
    )(done, right, left)


def solution(mesh):
    return jax.shard_map(
        functools.partial(per_device, mesh.shape["seg"]),
        mesh=mesh,
        in_specs=(P("chan", "seg"), P(), P(), P(), P()),
        out_specs=P("seg", None, None, "chan"),
        check_vma=False,
    )
```
